128 devices in a mesh: gx: 4 (over y), gy: 32 (over x, z, core).
Axes of the slice: x: 4, y: 4, z: 4, core: 2. Of those that a mesh axis runs over, the one named last changes fastest.
Arguments:
- positions: float32 [3, 2097152], P(None, ('gx', 'gy'))
- panel_weight: float32 [2097152], P(('gx', 'gy')), may hold values from 0.1 to 1
- charges: float32 [8, 2097152], P(None, ('gx', 'gy')), may hold values from -6 to 6
- basis: float32 [16, 2097152], P(None, ('gx', 'gy')), may hold values from -3 to 3
- proxies: float32 [3, 65536], P(None, ('gx', 'gy'))
- local_pairs: int32 [2, 4096], P(None, ('gx', 'gy')), may hold values from 0 to 31, as said below
- cross_pairs: int32 [2, 2048], P(None, ('gx', 'gy')), may hold values from 0 to 31, as said below
- cross_count: int32 [128], P(('gx', 'gy')), may hold values from 0 to 16, as said below
- far_blocks: int32 [2, 32768], P(None, ('gx', 'gy')), may hold values from 0 to 4095, as said below
Outputs:
- potential: float32 [8, 2097152], P(None, ('gx', 'gy'))
The draws below stay inside these ranges and needn't reach their ends.
Inputs may be any that keep to these rules, and one draw needn't show every extreme that they name: `local_pairs`: both rows hold local cluster indices and the first is smaller than the second. `cross_pairs`: the first row lies in 24 to 31 and the second in 0 to 7; slot 0 of every device pairs its cluster 32 - 1 with the next device's cluster 0. `cross_count`: at least 1 on every device but the last, which has 0; some device has 16. `far_blocks`: the first row holds local clusters, the second global clusters. A device's blocks are listed by owner: its blocks t * 2 to (t + 1) * 2 - 1 have row clusters owned by device t.
All inputs are finite; a program needn't handle non-finite values.
Results may differ from the reference program's by a relative error of at most 0.0003.
Values sent between devices are 32-bit elements; how exact they have to be, the bound alone decides.
A program may use at most 64 MiB of HBM per device.

```python
import math
import jax
import jax.numpy as jnp
from jax import lax

CLUSTER = 512
RANK = 16
RHS = 8
CL_DEV = 32
EDGE = 8
CROSS_DEV = 16
SLOT = 2
LOC_DEV = 32
FAR_DEV = 256
CLUSTERS = 4096
PANELS = 2097152
PROXIES = 65536
N_GX = 4
N_GY = 32


def cluster_centers(index):
    coord_x = jnp.zeros_like(index)
    coord_y = jnp.zeros_like(index)
    coord_z = jnp.zeros_like(index)
    for level in range(10):
        coord_x = coord_x + ((index >> 3 * level & 1) << level)
        coord_y = coord_y + ((index >> 3 * level + 1 & 1) << level)
        coord_z = coord_z + ((index >> 3 * level + 2 & 1) << level)
    return jnp.stack([coord_x, coord_y, coord_z]).astype(jnp.float32)


def draw_positions(key, part):
    key = jax.random.fold_in(key, 11)
    owner = jnp.arange(PANELS, dtype=jnp.int32) // CLUSTER
    centers = cluster_centers(owner)
    offsets = jnp.clip(0.25 * jax.random.normal(key, (3, PANELS), jnp.float32), -0.5, 0.5)
    return centers + offsets


def draw_proxies(key, part):
    key = jax.random.fold_in(key, 12)
    owner = jnp.arange(PROXIES, dtype=jnp.int32) // RANK
    centers = cluster_centers(owner)
    return centers + jax.random.uniform(key, (3, PROXIES), jnp.float32, -0.6, 0.6)


def draw_local_pairs(key, part):
    key = jax.random.fold_in(key, 13)
    key_first, key_gap = jax.random.split(key)
    count = LOC_DEV * (CLUSTERS // CL_DEV)
    first = jax.random.randint(key_first, (count,), 0, CL_DEV - 1)
    second = jnp.minimum(first + jax.random.randint(key_gap, (count,), 1, 5), CL_DEV - 1)
    return jnp.stack([first, second]).astype(jnp.int32)


def draw_cross_pairs(key, part):
    key = jax.random.fold_in(key, 14)
    key_first, key_second = jax.random.split(key)
    count = CROSS_DEV * (CLUSTERS // CL_DEV)
    first = CL_DEV - EDGE + jax.random.randint(key_first, (count,), 0, EDGE)
    second = jax.random.randint(key_second, (count,), 0, EDGE)
    leading = jnp.arange(count, dtype=jnp.int32) % CROSS_DEV == 0
    first = jnp.where(leading, CL_DEV - 1, first)
    second = jnp.where(leading, 0, second)
    return jnp.stack([first, second]).astype(jnp.int32)


def draw_cross_count(key, part):
    key = jax.random.fold_in(key, 15)
    key_counts, key_busy = jax.random.split(key)
    owners = CLUSTERS // CL_DEV
    counts = jax.random.randint(key_counts, (owners,), 1, CROSS_DEV + 1)
    busiest = jax.random.randint(key_busy, (), 0, owners - 1)
    counts = counts.at[busiest].set(CROSS_DEV)
    counts = counts.at[owners - 1].set(0)
    return counts.astype(jnp.int32)


def draw_far_blocks(key, part):
    key = jax.random.fold_in(key, 16)
    key_source, key_target = jax.random.split(key)
    count = FAR_DEV * (CLUSTERS // CL_DEV)
    source = jax.random.randint(key_source, (count,), 0, CL_DEV)
    owner = jnp.arange(count, dtype=jnp.int32) % FAR_DEV // SLOT
    local_row = jax.random.randint(key_target, (count,), 0, CL_DEV)
    local_row = local_row.at[count - 1].set(CL_DEV - 1)
    source = source.at[0].set(CL_DEV - 1)
    target = owner * CL_DEV + local_row
    return jnp.stack([source, target]).astype(jnp.int32)


def level_of(key, extent, cuts, smallest, top_value):
    factor_of = 1.0
    for position, parts in cuts:
        draws = jax.random.uniform(jax.random.fold_in(jax.random.fold_in(key, 6), position), (parts,), jnp.float32, smallest / len(cuts), top_value / len(cuts))
        factor_of = factor_of * jnp.repeat(jnp.exp(draws), extent[position] // parts).reshape((-1,) + (1,) * (len(extent) - 1 - position))
    return factor_of


def normal_values(rng, shape, deviation, limit, cuts=(), kind=jnp.bfloat16):
    gain = level_of(rng, shape, cuts, -0.22, 0.18) if cuts else 1.0
    values = jax.random.normal(rng, shape, jnp.float32) * deviation * gain
    return jnp.minimum(jnp.maximum(values, -limit), limit).astype(kind)


def setup_inputs(seed: int = 0) -> dict:
    key_of = jax.random.split(jax.random.key(seed), 10)
    return {
        "positions": draw_positions(jax.random.fold_in(key_of[9], 71), 0),
        "panel_weight": jnp.clip(jnp.exp(math.log(1.0) - 2.3025851 * jax.random.uniform(key_of[1], (PANELS,), jnp.float32) ** level_of(key_of[1], (PANELS,), ((0, 128),), -0.2, 0.2)), 0.1, 1.0),
        "charges": normal_values(key_of[2], (RHS, PANELS), 1.0, 6.0, ((1, 128),), jnp.float32),
        "basis": normal_values(key_of[3], (RANK, PANELS), 0.5, 3.0, ((1, 128),), jnp.float32),
        "proxies": draw_proxies(jax.random.fold_in(key_of[9], 71), 0),
        "local_pairs": draw_local_pairs(jax.random.fold_in(key_of[9], 71), 0),
        "cross_pairs": draw_cross_pairs(jax.random.fold_in(key_of[9], 71), 0),
        "cross_count": draw_cross_count(jax.random.fold_in(key_of[9], 71), 0),
        "far_blocks": draw_far_blocks(jax.random.fold_in(key_of[9], 71), 0),
    }


FOUR_PI_INV = 0.07957747154594767
SOFTENING = 0.0025
batch_tiles = 16

def reference(positions, panel_weight, charges, basis, proxies, local_pairs, cross_pairs, cross_count, far_blocks):
    devices = N_GX * N_GY
    clusters = CL_DEV * devices
    highest = lax.Precision.HIGHEST
    weighted = charges * panel_weight[None, :]
    pos_blocks = positions.reshape(3, clusters, CLUSTER)
    charge_blocks = weighted.reshape(RHS, clusters, CLUSTER)
    self_index = jnp.arange(clusters, dtype=jnp.int32)
    local_owner = jnp.arange(LOC_DEV * devices, dtype=jnp.int32) // LOC_DEV * CL_DEV
    cross_slot = jnp.arange(CROSS_DEV * devices, dtype=jnp.int32)
    cross_owner = cross_slot // CROSS_DEV
    cross_live = (cross_slot % CROSS_DEV < cross_count[cross_owner]).astype(jnp.float32)
    next_owner = jnp.minimum(cross_owner + 1, devices - 1)
    first = jnp.concatenate([self_index, local_owner + local_pairs[0], cross_owner * CL_DEV + cross_pairs[0]]).astype(jnp.int32)
    second = jnp.concatenate([self_index, local_owner + local_pairs[1], next_owner * CL_DEV + cross_pairs[1]]).astype(jnp.int32)
    twice = jnp.concatenate([jnp.zeros((clusters,), jnp.float32), jnp.ones((LOC_DEV * devices,), jnp.float32), jnp.ones((CROSS_DEV * devices,), jnp.float32)])
    alive = jnp.concatenate([jnp.ones((clusters + LOC_DEV * devices,), jnp.float32), cross_live])
    total = first.shape[0]
    padding = -total % batch_tiles
    first = jnp.concatenate([first, jnp.zeros((padding,), jnp.int32)]).reshape(-1, batch_tiles)
    second = jnp.concatenate([second, jnp.zeros((padding,), jnp.int32)]).reshape(-1, batch_tiles)
    twice = jnp.concatenate([twice, jnp.zeros((padding,), jnp.float32)]).reshape(-1, batch_tiles)
    alive = jnp.concatenate([alive, jnp.zeros((padding,), jnp.float32)]).reshape(-1, batch_tiles)

    def apply_batch(near, item):
        idx_first, idx_second, twice_b, alive_b = item
        pos_first = pos_blocks[:, idx_first]
        pos_second = pos_blocks[:, idx_second]
        dist_sq = lax.optimization_barrier(jnp.sum((pos_first[:, :, :, None] - pos_second[:, :, None, :]) ** 2, axis=0))
        tile = FOUR_PI_INV * lax.rsqrt(dist_sq + SOFTENING) * alive_b[:, None, None]
        to_first = jnp.einsum('rbq,bpq->rbp', charge_blocks[:, idx_second], tile, precision=highest)
        to_second = jnp.einsum('rbp,bpq->rbq', charge_blocks[:, idx_first], tile, precision=highest) * twice_b[None, :, None]
        near = near.at[:, idx_first].add(to_first)
        near = near.at[:, idx_second].add(to_second)
        return (near, None)
    near, _ = lax.scan(apply_batch, jnp.zeros((RHS, clusters, CLUSTER), jnp.float32), (first, second, twice, alive))
    basis_blocks = basis.reshape(RANK, clusters, CLUSTER)
    coef = jnp.einsum('kcn,rcn->ckr', basis_blocks, charge_blocks, precision=highest)
    proxy_blocks = proxies.reshape(3, clusters, RANK)
    block_owner = jnp.arange(FAR_DEV * devices, dtype=jnp.int32) // FAR_DEV
    source = (block_owner * CL_DEV + far_blocks[0]).astype(jnp.int32)
    target = far_blocks[1].astype(jnp.int32)
    target_proxy = proxy_blocks[:, target]
    source_proxy = proxy_blocks[:, source]
    dist_far = lax.optimization_barrier(jnp.sum((target_proxy[:, :, :, None] - source_proxy[:, :, None, :]) ** 2, axis=0))
    coupling = FOUR_PI_INV * lax.rsqrt(dist_far + SOFTENING)
    contrib = jnp.einsum('bkl,blr->bkr', coupling, coef[source], precision=highest)
    rowcoef = jnp.zeros((clusters, RANK, RHS), jnp.float32).at[target].add(contrib)
    far = jnp.einsum('kcn,ckr->rcn', basis_blocks, rowcoef, precision=highest)
    return panel_weight[None, :] * (near + far).reshape(RHS, clusters * CLUSTER)
```

```python
import functools

import jax
import jax.numpy as jnp
from jax import lax
from jax.experimental import pallas as pl
from jax.experimental.pallas import tpu as pltpu
from jax.sharding import PartitionSpec as P

CLUSTER = 512
RANK = 16
RHS = 8
EDGE = 8
FOUR_PI_INV = 0.07957747154594767
SOFTENING = 0.0025
CL_DEV = 32
LOC_DEV = 32
CROSS_DEV = 16
FAR_DEV = 256
EDGE_PANELS = EDGE * CLUSTER
CHUNK = 32
DEVICES = 128
N_Y, N_X, N_ZC = 4, 4, 8
ROWS = 8
MESH = pl.DeviceIdType.MESH
F32 = jnp.float32
BF16 = jnp.bfloat16


def dot(a, b, dims):
    return lax.dot_general(a, b, ((dims[:1], dims[1:]), ((), ())), preferred_element_type=F32)


def split(value, parts):
    out = []
    for _ in range(parts - 1):
        high = value.astype(BF16)
        out.append(high)
        value = value - high.astype(F32)
    out.append(value.astype(BF16))
    return out


def panels_of(cluster):
    return pl.ds(pl.multiple_of(cluster * CLUSTER, CLUSTER), CLUSTER)


def split_rows(value):
    high = value.astype(BF16).astype(F32)
    return jnp.concatenate([high, value - high], axis=0).astype(BF16)


def near_kernel(
    pos, weight, charges, basis, proxy_table, ids, local_pairs, cross_pairs, cross_mask,
    self_sum, first_sum, second_sum, cross_sum, far_in, returned,
    cw, pos_c, pos_t, moments, send, recv1, recv2, head_w, next_pos, next_w, next_pos_c, next_cw, back, tile_hi, tile_lo,
    far_send, far_recv, far_own, edge_send, edge_recv,
):
    y = lax.axis_index("gx")
    gy = lax.axis_index("gy")
    x = gy // N_ZC
    zc = lax.rem(gy, N_ZC)
    flat = y * (N_X * N_ZC) + gy

    def device_of(index):
        return (index // (N_X * N_ZC), lax.rem(index, N_X * N_ZC))

    after = device_of(lax.rem(flat + 1, DEVICES))
    before = device_of(lax.rem(flat + DEVICES - 1, DEVICES))
    peers = (
        [(lax.rem(y + i, N_Y), gy) for i in range(1, N_Y)]
        + [(y, lax.rem(x + i, N_X) * N_ZC + zc) for i in range(1, N_X)]
        + [(y, x * N_ZC + lax.rem(zc + i, N_ZC)) for i in range(1, N_ZC)]
    )
    barrier = pltpu.get_barrier_semaphore()
    for peer in peers + [after, before]:
        pl.semaphore_signal(barrier, inc=1, device_id=peer, device_id_type=MESH)

    def prepare(c, carry):
        cols = panels_of(c)
        weighted = charges[:, cols] * weight[:, cols]
        parts = split_rows(weighted)
        cw[c] = parts
        place = jnp.concatenate([pos[:, cols], jnp.zeros((5, CLUSTER), F32)], axis=0)
        pos_c[c] = place
        pos_t[c] = place.T
        moments[pl.ds(pl.multiple_of(c * 32, 32), 32), :] = dot(split_rows(basis[:, cols]), parts, (1, 1))
        return carry

    lax.fori_loop(0, CL_DEV, prepare, 0)
    head_w[...] = charges[:, :EDGE_PANELS] * weight[:, :EDGE_PANELS]

    row = lax.broadcasted_iota(jnp.int32, (2 * RHS, 128), 0)
    lane = lax.broadcasted_iota(jnp.int32, (2 * RHS, 128), 1)
    spread = jnp.where(lax.rem(row, RHS) == lax.rem(lane, RHS), 1.0, 0.0).astype(BF16)
    wide = sum(dot(part, spread, (1, 0)) for part in split(moments[...], 3))
    row = lax.broadcasted_iota(jnp.int32, wide.shape, 0)
    lane = lax.broadcasted_iota(jnp.int32, wide.shape, 1)
    wide = jnp.where(lax.rem(row, RANK) == lane // RHS, wide, 0.0)
    coef = jnp.sum(wide.reshape(CL_DEV, 2 * RANK, 128), axis=1)

    coef_parts = split(coef, 3)
    proxy_parts = split(proxy_table[...], 3)
    row = lax.broadcasted_iota(jnp.int32, (32, 128), 0)
    lane = lax.broadcasted_iota(jnp.int32, (32, 128), 1)
    numbers = jnp.where(lane == 3 * RANK, row.astype(F32), 0.0).astype(BF16)
    table = jnp.concatenate(
        [coef_parts[0], proxy_parts[0], coef_parts[1], proxy_parts[1], coef_parts[2], proxy_parts[2], numbers],
        axis=0,
    )
    row = lax.broadcasted_iota(jnp.int32, (192, 1), 0)
    pick_table = jnp.where(lax.rem(row, 64) == ids[0:1, :], 1.0, 0.0)
    row = lax.broadcasted_iota(jnp.int32, (32, 1), 0)
    pick_number = jnp.where(row == ids[1:2, :], 1.0, 0.0)
    pick = jnp.concatenate([pick_table, pick_number], axis=0).astype(BF16)
    send[...] = dot(pick, table, (0, 0)).reshape(send.shape)

    def far_copy(source, target, index, peer):
        return pltpu.make_async_remote_copy(
            src_ref=source, dst_ref=target, send_sem=far_send.at[index], recv_sem=far_recv.at[index],
            device_id=peer, device_id_type=MESH,
        )

    def edge_copy(source, target, index, peer):
        return pltpu.make_async_remote_copy(
            src_ref=source, dst_ref=target, send_sem=edge_send.at[index], recv_sem=edge_recv.at[index],
            device_id=peer, device_id_type=MESH,
        )

    def start(copies):
        for copy in copies:
            copy.start()

    def wait(copies):
        for copy in copies:
            copy.wait()

    phase1 = [pltpu.make_async_copy(send.at[y], recv1.at[0], far_own.at[0])] + [
        far_copy(send.at[lax.rem(y + i, N_Y)], recv1.at[i], i - 1, peers[i - 1]) for i in range(1, N_Y)
    ]
    phase2 = [pltpu.make_async_copy(recv1.at[:, x], recv2.at[0], far_own.at[1])] + [
        far_copy(recv1.at[:, lax.rem(x + i, N_X)], recv2.at[i], 2 + i, peers[2 + i]) for i in range(1, N_X)
    ]
    phase3 = [pltpu.make_async_copy(recv2.at[:, :, zc], far_in.at[0], far_own.at[2])] + [
        far_copy(recv2.at[:, :, lax.rem(zc + i, N_ZC)], far_in.at[i], 5 + i, peers[5 + i]) for i in range(1, N_ZC)
    ]
    heads = [
        edge_copy(pos.at[:, pl.ds(0, EDGE_PANELS)], next_pos, 0, before),
        edge_copy(head_w, next_w, 1, before),
    ]
    give_back = [edge_copy(back, returned, 2, after)]

    pl.semaphore_wait(barrier, len(peers) + 2)
    start(heads)
    start(phase1)

    def tile(row_cluster, columns, slot):
        col_x, col_y, col_z = columns[0:1, :], columns[1:2, :], columns[2:3, :]
        for i in range(CLUSTER // CHUNK):
            rows = pos_t[row_cluster, i * CHUNK : (i + 1) * CHUNK, :]
            dx = rows[:, 0:1] - col_x
            dy = rows[:, 1:2] - col_y
            dz = rows[:, 2:3] - col_z
            value = lax.rsqrt(dx * dx + dy * dy + dz * dz + SOFTENING)
            high = value.astype(BF16)
            tile_hi[slot, i * CHUNK : (i + 1) * CHUNK, :] = high
            tile_lo[slot, i * CHUNK : (i + 1) * CHUNK, :] = (value - high.astype(F32)).astype(BF16)

    def applied(parts, slot, side):
        sums = dot(parts, tile_hi[slot], (1, side)) + dot(parts, tile_lo[slot], (1, side))
        return sums[:RHS] + sums[RHS:]

    def section(count, compute, apply):
        compute(0, 0)

        def body(i, carry):
            compute(2 * i + 1, 1)
            apply(2 * i, 0)
            compute(jnp.minimum(2 * i + 2, count - 1), 0)
            apply(2 * i + 1, 1)
            return carry

        lax.fori_loop(0, count // 2, body, 0)

    def self_compute(t, slot):
        tile(t, pos_c[t], slot)

    def self_apply(t, slot):
        self_sum[:, panels_of(t)] = applied(cw[t], slot, 0)

    section(CL_DEV, self_compute, self_apply)

    wait(phase1)
    start(phase2)
    wait(heads)
    for j in range(EDGE):
        cols = slice(j * CLUSTER, (j + 1) * CLUSTER)
        next_cw[j] = split_rows(next_w[:, cols])
        next_pos_c[j, 0:3, :] = next_pos[:, cols]
    back[...] = jnp.zeros_like(back)

    def cross_compute(t, slot):
        tile(cross_pairs[0, t], next_pos_c[cross_pairs[1, t]], slot)

    def cross_apply(t, slot):
        cross_sum[t] = applied(next_cw[cross_pairs[1, t]], slot, 1) * cross_mask[EDGE, t]
        product = applied(cw[cross_pairs[0, t]], slot, 0)
        for j in range(EDGE):
            back[j] += product * cross_mask[j, t]

    section(CROSS_DEV, cross_compute, cross_apply)
    start(give_back)
    wait(phase2)
    start(phase3)

    def local_compute(t, slot):
        tile(local_pairs[0, t], pos_c[local_pairs[1, t]], slot)

    def local_apply(t, slot):
        first_sum[t] = applied(cw[local_pairs[1, t]], slot, 1)
        second_sum[t] = applied(cw[local_pairs[0, t]], slot, 0)

    section(LOC_DEV, local_compute, local_apply)
    wait(phase3)
    wait(give_back)


def far_kernel(
    far_in, proxy_table, basis, weight, self_sum, first_sum, second_sum, cross_sum, returned,
    local_pairs, cross_pairs, out, rows_ref,
):
    def strided(j):
        return far_in[pl.ds(j, DEVICES, stride=ROWS), :]

    coef = jnp.concatenate([strided(0), strided(1)], axis=0)
    source = jnp.concatenate([strided(2), strided(3)], axis=0)
    lane = lax.broadcasted_iota(jnp.int32, (FAR_DEV, 128), 1)
    number = jnp.sum(jnp.where(lane == 3 * RANK, source, 0.0), axis=1, keepdims=True).astype(jnp.int32)
    lane = lax.broadcasted_iota(jnp.int32, (FAR_DEV, CL_DEV), 1)
    pick = jnp.where(lane == number, 1.0, 0.0).astype(BF16)
    target = sum(dot(pick, part, (1, 0)) for part in split(proxy_table[...], 3))
    row = lax.broadcasted_iota(jnp.int32, (128, 3 * 256), 0)
    lane = lax.broadcasted_iota(jnp.int32, (128, 3 * 256), 1)
    axis = lane // 256
    from_target = jnp.where(row == axis * RANK + lax.rem(lane, 256) // RANK, 1.0, 0.0).astype(BF16)
    from_source = jnp.where(row == axis * RANK + lax.rem(lane, RANK), -1.0, 0.0).astype(BF16)
    offsets = sum(dot(part, from_target, (1, 0)) for part in split(target, 3))
    offsets = offsets + sum(dot(part, from_source, (1, 0)) for part in split(source, 3))
    offsets = offsets * offsets
    coupling = lax.rsqrt(offsets[:, :256] + offsets[:, 256:512] + offsets[:, 512:] + SOFTENING)
    coupling_parts = split(coupling, 2)
    coef_parts = split(coef, 2)
    contrib = jnp.zeros((FAR_DEV, 128), F32)
    for l in range(RANK):
        row = lax.broadcasted_iota(jnp.int32, (256, 128), 0)
        lane = lax.broadcasted_iota(jnp.int32, (256, 128), 1)
        widen = jnp.where(row == (lane // RHS) * RANK + l, 1.0, 0.0).astype(BF16)
        row = lax.broadcasted_iota(jnp.int32, (128, 128), 0)
        lane = lax.broadcasted_iota(jnp.int32, (128, 128), 1)
        repeat = jnp.where(row == l * RHS + lax.rem(lane, RHS), 1.0, 0.0).astype(BF16)
        left = sum(dot(part, widen, (1, 0)) for part in coupling_parts)
        right = sum(dot(part, repeat, (1, 0)) for part in coef_parts)
        contrib = contrib + left * right
    rowcoef = sum(dot(pick, part, (0, 0)) for part in split(contrib, 3))
    row = lax.broadcasted_iota(jnp.int32, (CL_DEV * RHS, CL_DEV), 0)
    lane = lax.broadcasted_iota(jnp.int32, (CL_DEV * RHS, CL_DEV), 1)
    eight = jnp.where(row // RHS == lane, 1.0, 0.0).astype(BF16)
    wide = sum(dot(eight, part, (1, 0)) for part in split(rowcoef, 3))
    row = lax.broadcasted_iota(jnp.int32, wide.shape, 0)
    lane = lax.broadcasted_iota(jnp.int32, wide.shape, 1)
    wide = jnp.where(lax.rem(row, RHS) == lax.rem(lane, RHS), wide, 0.0)
    row = lax.broadcasted_iota(jnp.int32, (128, RANK), 0)
    lane = lax.broadcasted_iota(jnp.int32, (128, RANK), 1)
    narrow = jnp.where(row // RHS == lane, 1.0, 0.0).astype(BF16)
    rows_ref[...] = sum(dot(part, narrow, (1, 0)) for part in split(wide, 3))

    def start(c, carry):
        cols = panels_of(c)
        block = basis[:, cols]
        high = block.astype(BF16).astype(F32)
        blocks = jnp.concatenate([high, block - high, high], axis=0).astype(BF16)
        left = rows_ref[pl.ds(pl.multiple_of(c * RHS, RHS), RHS), :]
        left_high = left.astype(BF16).astype(F32)
        lefts = jnp.concatenate([left_high, left_high, left - left_high], axis=1).astype(BF16)
        out[:, cols] = self_sum[:, cols] + dot(lefts, blocks, (1, 0))
        return carry

    lax.fori_loop(0, CL_DEV, start, 0)
    for j in range(EDGE):
        out[:, j * CLUSTER : (j + 1) * CLUSTER] += returned[j]

    def add_local(t, carry):
        out[:, panels_of(local_pairs[0, t])] += first_sum[t]
        out[:, panels_of(local_pairs[1, t])] += second_sum[t]
        return carry

    lax.fori_loop(0, LOC_DEV, add_local, 0)

    def add_cross(t, carry):
        out[:, panels_of(cross_pairs[0, t])] += cross_sum[t]
        return carry

    lax.fori_loop(0, CROSS_DEV, add_cross, 0)
    out[...] = out[...] * (weight[...] * FOUR_PI_INV)


def on_device(
    positions, panel_weight, charges, basis, proxies, local_pairs, cross_pairs, cross_count, far_blocks
):
    panels = positions.shape[1]
    weight = panel_weight.reshape(1, panels)
    proxy_table = proxies.reshape(3, CL_DEV, RANK).transpose(1, 0, 2).reshape(CL_DEV, 3 * RANK)
    proxy_table = jnp.pad(proxy_table, ((0, 0), (0, 128 - 3 * RANK)))
    source = far_blocks[0].reshape(DEVICES, 2)
    local_row = lax.rem(far_blocks[1], CL_DEV).reshape(DEVICES, 2)
    none = jnp.full((DEVICES, 2), -1, jnp.int32)
    table_ids = jnp.concatenate([source, source + CL_DEV, none, none], axis=1).reshape(1, -1)
    number_ids = jnp.concatenate([none, local_row, none, none], axis=1).reshape(1, -1)
    ids = jnp.concatenate([table_ids, number_ids], axis=0)
    alive = jnp.arange(CROSS_DEV, dtype=jnp.int32)[None, :] < cross_count[0]
    edge = jnp.arange(EDGE + 1, dtype=jnp.int32)[:, None]
    cross_mask = ((edge == cross_pairs[1:2, :]) | (edge == EDGE)) & alive
    cross_mask = cross_mask.astype(F32)

    vmem = pl.BlockSpec(memory_space=pltpu.VMEM)
    smem = pl.BlockSpec(memory_space=pltpu.SMEM)
    block = functools.partial(pltpu.VMEM, dtype=F32)
    outs = pl.pallas_call(
        near_kernel,
        out_shape=[
            jax.ShapeDtypeStruct(shape, F32)
            for shape in (
                (RHS, panels),
                (LOC_DEV, RHS, CLUSTER),
                (LOC_DEV, RHS, CLUSTER),
                (CROSS_DEV, RHS, CLUSTER),
                (N_ZC, N_X, N_Y, ROWS, 128),
                (EDGE, RHS, CLUSTER),
            )
        ],
        in_specs=[vmem] * 6 + [smem] * 3,
        out_specs=[vmem] * 6,
        scratch_shapes=[
            pltpu.VMEM((CL_DEV, 2 * RHS, CLUSTER), BF16),
            pltpu.VMEM((CL_DEV, 8, CLUSTER), F32),
            pltpu.VMEM((CL_DEV, CLUSTER, 8), F32),
            pltpu.VMEM((CL_DEV * 2 * RANK, 2 * RHS), F32),
            pltpu.VMEM((N_Y, N_X, N_ZC, ROWS, 128), F32),
            pltpu.VMEM((N_Y, N_X, N_ZC, ROWS, 128), F32),
            pltpu.VMEM((N_X, N_Y, N_ZC, ROWS, 128), F32),
            pltpu.VMEM((RHS, EDGE_PANELS), F32),
            pltpu.VMEM((3, EDGE_PANELS), F32),
            pltpu.VMEM((RHS, EDGE_PANELS), F32),
            pltpu.VMEM((EDGE, 8, CLUSTER), F32),
            pltpu.VMEM((EDGE, 2 * RHS, CLUSTER), BF16),
            pltpu.VMEM((EDGE, RHS, CLUSTER), F32),
            pltpu.VMEM((2, CLUSTER, CLUSTER), BF16),
            pltpu.VMEM((2, CLUSTER, CLUSTER), BF16),
            pltpu.SemaphoreType.DMA((13,)),
            pltpu.SemaphoreType.DMA((13,)),
            pltpu.SemaphoreType.DMA((3,)),
            pltpu.SemaphoreType.DMA((3,)),
            pltpu.SemaphoreType.DMA((3,)),
        ],
        compiler_params=pltpu.CompilerParams(
            collective_id=0, has_side_effects=True, vmem_limit_bytes=48 * 2**20
        ),
    )(positions, weight, charges, basis, proxy_table, ids, local_pairs, cross_pairs, cross_mask)
    self_sum, first_sum, second_sum, cross_sum, far_in, returned = outs
    return pl.pallas_call(
        far_kernel,
        out_shape=jax.ShapeDtypeStruct((RHS, panels), F32),
        in_specs=[vmem] * 9 + [smem] * 2,
        out_specs=vmem,
        scratch_shapes=[pltpu.VMEM((CL_DEV * RHS, RANK), F32)],
        compiler_params=pltpu.CompilerParams(vmem_limit_bytes=48 * 2**20),
    )(
        far_in.reshape(-1, 128), proxy_table, basis, weight, self_sum, first_sum, second_sum, cross_sum,
        returned, local_pairs, cross_pairs,
    )


def solution(mesh):
    whole = P(None, ("gx", "gy"))
    flat = P(("gx", "gy"))
    return jax.shard_map(
        on_device,
        mesh=mesh,
        in_specs=(whole, flat, whole, whole, whole, whole, whole, flat, whole),
        out_specs=whole,
        check_vma=False,
    )
```

```python
import functools

import jax
import jax.numpy as jnp
from jax import lax
from jax.experimental import pallas as pl
from jax.experimental.pallas import tpu as pltpu
from jax.sharding import PartitionSpec as P

CLUSTER = 512
RANK = 16
RHS = 8
EDGE = 8
FOUR_PI_INV = 0.07957747154594767
SOFTENING = 0.0025
CL_DEV = 32
LOC_DEV = 32
CROSS_DEV = 16
PAIRS = CROSS_DEV + LOC_DEV
FAR_DEV = 256
EDGE_PANELS = EDGE * CLUSTER
CHUNK = 32
STRIP = 128
DEVICES = 128
N_Y, N_X, N_ZC = 4, 4, 8
ROWS = 8
MESH = pl.DeviceIdType.MESH
F32 = jnp.float32
BF16 = jnp.bfloat16


def dot(a, b, dims):
    return lax.dot_general(a, b, ((dims[:1], dims[1:]), ((), ())), preferred_element_type=F32)


def split(value, parts):
    out = []
    for _ in range(parts - 1):
        high = value.astype(BF16)
        out.append(high)
        value = value - high.astype(F32)
    out.append(value.astype(BF16))
    return out


def split_rows(value):
    high = value.astype(BF16).astype(F32)
    return jnp.concatenate([high, value - high], axis=0).astype(BF16)


def iotas(shape):
    return lax.broadcasted_iota(jnp.int32, shape, 0), lax.broadcasted_iota(jnp.int32, shape, 1)


def ones_where(condition):
    return jnp.where(condition, 1.0, 0.0).astype(BF16)


def cluster_cols(c):
    return slice(c * CLUSTER, (c + 1) * CLUSTER)


def near_kernel(
    pos_hbm, weight_hbm, charges_hbm, basis_hbm, proxies, far_blocks, cross_vector, local_pairs, cross_pairs, cross_count,
    self_sum, first_sum, second_sum, far_in, returned, info_in, proxy_table,
    pos, weight, charges, basis, cw, pos_c, pos_t, moments, coef_rows, proxy_rows, send, recv1, recv2, head_w, next_pos, next_w,
    info, hi0, hi1, lo0, lo1, load_sem, far_send, far_recv, far_own, edge_send, edge_recv,
):
    y = lax.axis_index("gx")
    gy = lax.axis_index("gy")
    x = gy // N_ZC
    zc = lax.rem(gy, N_ZC)
    flat = y * (N_X * N_ZC) + gy
    tile_hi, tile_lo = (hi0, hi1), (lo0, lo1)

    loads = [
        pltpu.make_async_copy(source, target, load_sem.at[i])
        for i, (source, target) in enumerate(
            ((weight_hbm, weight), (charges_hbm, charges), (pos_hbm, pos), (basis_hbm, basis))
        )
    ]
    for load in loads:
        load.start()

    def device_of(index):
        return (index // (N_X * N_ZC), lax.rem(index, N_X * N_ZC))

    after = device_of(lax.rem(flat + 1, DEVICES))
    before = device_of(lax.rem(flat + DEVICES - 1, DEVICES))
    peers = (
        [(lax.rem(y + i, N_Y), gy) for i in range(1, N_Y)]
        + [(y, lax.rem(x + i, N_X) * N_ZC + zc) for i in range(1, N_X)]
        + [(y, x * N_ZC + lax.rem(zc + i, N_ZC)) for i in range(1, N_ZC)]
    )
    barrier = pltpu.get_barrier_semaphore()
    for peer in peers + [after, before]:
        pl.semaphore_signal(barrier, inc=1, device_id=peer, device_id_type=MESH)

    info[...] = jnp.zeros_like(info)
    info[0:2, 0:CROSS_DEV] = cross_vector[...]
    info[2:3, :] = jnp.full((1, 128), cross_count[0], jnp.int32)

    columns = jnp.concatenate([proxies[...], jnp.zeros((5, CL_DEV * RANK), F32)], axis=0).T
    row, lane = iotas((CL_DEV * RANK, 128))
    spread = jnp.where(
        lane < RANK, columns[:, 0:1], jnp.where(lane < 2 * RANK, columns[:, 1:2], columns[:, 2:3])
    )
    spread = jnp.where((lax.rem(row, RANK) == lax.rem(lane, RANK)) & (lane < 3 * RANK), spread, 0.0)
    row, lane = iotas((CL_DEV, CL_DEV * RANK))
    gather = ones_where(row == lane // RANK)
    table = sum(dot(gather, part, (1, 0)) for part in split(spread, 3))
    proxy_table[...] = table

    for load in loads:
        load.wait()
    for c in range(CL_DEV):
        cols = cluster_cols(c)
        parts = split_rows(charges[:, cols] * weight[:, cols])
        cw[c] = parts
        place = jnp.concatenate([pos[:, cols], jnp.zeros((5, CLUSTER), F32)], axis=0)
        pos_c[c] = place
        pos_t[c] = place.T
        moments[c * 32 : (c + 1) * 32, :] = dot(split_rows(basis[:, cols]), parts, (1, 1))
    head_w[...] = charges[:, :EDGE_PANELS] * weight[:, :EDGE_PANELS]

    row, lane = iotas((2 * RHS, 128))
    spread = ones_where(lax.rem(row, RHS) == lax.rem(lane, RHS))
    wide = sum(dot(part, spread, (1, 0)) for part in split(moments[...], 3))
    row, lane = iotas(wide.shape)
    wide = jnp.where(lax.rem(row, RANK) == lane // RHS, wide, 0.0)
    coef = jnp.sum(wide.reshape(CL_DEV, 2 * RANK, 128), axis=1)

    row, lane = iotas((CL_DEV, 256))
    numbers = jnp.where(lane == 128 + 3 * RANK, row.astype(F32), 0.0).astype(BF16)
    both = jnp.concatenate(split(jnp.concatenate([coef, table], axis=1), 3) + [numbers], axis=0)
    row, lane = iotas((3 * CL_DEV, FAR_DEV))
    pick_source = jnp.where(lax.rem(row, CL_DEV) == far_blocks[0:1, :], 1.0, 0.0)
    row, lane = iotas((CL_DEV, FAR_DEV))
    pick_number = jnp.where(row == (far_blocks[1:2, :] & (CL_DEV - 1)), 1.0, 0.0)
    pick = jnp.concatenate([pick_source, pick_number], axis=0).astype(BF16)
    picked = dot(pick, both, (0, 0))
    coef_rows[...] = picked[:, :128]
    proxy_rows[...] = picked[:, 128:]
    for j in range(2):
        send[pl.ds(j, DEVICES, stride=ROWS), :] = coef_rows[pl.ds(j, DEVICES, stride=2), :]
        for k in range(2, ROWS, 2):
            send[pl.ds(k + j, DEVICES, stride=ROWS), :] = proxy_rows[pl.ds(j, DEVICES, stride=2), :]

    def far_copy(source, target, index, peer):
        return pltpu.make_async_remote_copy(
            src_ref=source, dst_ref=target, send_sem=far_send.at[index], recv_sem=far_recv.at[index],
            device_id=peer, device_id_type=MESH,
        )

    def edge_copy(source, target, index, peer):
        return pltpu.make_async_remote_copy(
            src_ref=source, dst_ref=target, send_sem=edge_send.at[index], recv_sem=edge_recv.at[index],
            device_id=peer, device_id_type=MESH,
        )

    def start(copies):
        for copy in copies:
            copy.start()

    def wait(copies):
        for copy in copies:
            copy.wait()

    def part(index, count):
        return pl.ds(pl.multiple_of(index * count, count), count)

    per_y, per_x = N_X * N_ZC * ROWS, N_ZC * ROWS
    phase1 = [pltpu.make_async_copy(send.at[part(y, per_y)], recv1.at[0], far_own.at[0])] + [
        far_copy(send.at[part(lax.rem(y + i, N_Y), per_y)], recv1.at[i], i - 1, peers[i - 1])
        for i in range(1, N_Y)
    ]
    phase2 = [pltpu.make_async_copy(recv1.at[:, part(x, per_x)], recv2.at[0], far_own.at[1])] + [
        far_copy(recv1.at[:, part(lax.rem(x + i, N_X), per_x)], recv2.at[i], 2 + i, peers[2 + i])
        for i in range(1, N_X)
    ]
    phase3 = [pltpu.make_async_copy(recv2.at[:, :, part(zc, ROWS)], far_in.at[0], far_own.at[2])] + [
        far_copy(recv2.at[:, :, part(lax.rem(zc + i, N_ZC), ROWS)], far_in.at[i], 5 + i, peers[5 + i])
        for i in range(1, N_ZC)
    ]
    heads = [
        edge_copy(pos.at[:, pl.ds(0, EDGE_PANELS)], next_pos, 0, before),
        edge_copy(head_w, next_w, 1, before),
        edge_copy(info, info_in, 2, after),
    ]
    give_back = [edge_copy(second_sum.at[pl.ds(0, CROSS_DEV)], returned, 3, after)]

    pl.semaphore_wait(barrier, len(peers) + 2)
    start(heads)
    start(phase1)

    def fill(row_cluster, columns, slot, row_from, row_to, col_from):
        col_x = columns[0:1, col_from:]
        col_y = columns[1:2, col_from:]
        col_z = columns[2:3, col_from:]
        for begin in range(row_from, row_to, CHUNK):
            rows = pos_t[row_cluster, begin : begin + CHUNK, :]
            dx = rows[:, 0:1] - col_x
            dy = rows[:, 1:2] - col_y
            dz = rows[:, 2:3] - col_z
            value = lax.rsqrt(dx * dx + dy * dy + dz * dz + SOFTENING)
            high = value.astype(BF16)
            tile_hi[slot][begin : begin + CHUNK, col_from:] = high
            tile_lo[slot][begin : begin + CHUNK, col_from:] = (value - high.astype(F32)).astype(BF16)

    def halves(parts, slot, rows, cols, side):
        sums = dot(parts, tile_hi[slot][rows, cols], (1, side)) + dot(parts, tile_lo[slot][rows, cols], (1, side))
        return sums[:RHS] + sums[RHS:]

    whole = slice(0, CLUSTER)

    def self_compute(t, slot):
        columns = pos_c[t]
        for begin in range(0, CLUSTER, STRIP):
            fill(t, columns, slot, begin, begin + STRIP, begin)

    def self_apply(t, slot):
        parts = cw[t]
        sums = [None] * (CLUSTER // STRIP)
        for i in range(CLUSTER // STRIP):
            rows = slice(i * STRIP, (i + 1) * STRIP)
            down = halves(parts[:, rows], slot, rows, slice(i * STRIP, CLUSTER), 0)
            for j in range(i, CLUSTER // STRIP):
                piece = down[:, (j - i) * STRIP : (j - i + 1) * STRIP]
                sums[j] = piece if sums[j] is None else sums[j] + piece
            if i + 1 < CLUSTER // STRIP:
                rest = slice((i + 1) * STRIP, CLUSTER)
                sums[i] = sums[i] + halves(parts[:, rest], slot, rows, rest, 1)
        self_sum[t] = jnp.concatenate(sums, axis=1)

    def pair_of(t):
        crossing = t < CROSS_DEV
        c, l = jnp.minimum(t, CROSS_DEV - 1), jnp.maximum(t - CROSS_DEV, 0)
        first = jnp.where(crossing, cross_pairs[0, c], local_pairs[0, l])
        second = jnp.where(crossing, cross_pairs[1, c] + CL_DEV, local_pairs[1, l])
        return first, second

    def pair_compute(t, slot):
        first, second = pair_of(t)
        fill(first, pos_c[second], slot, 0, CLUSTER, 0)

    def pair_apply(t, slot):
        first, second = pair_of(t)
        first_sum[t] = halves(cw[second], slot, whole, whole, 1)
        second_sum[t] = halves(cw[first], slot, whole, whole, 0)

    def section(count, compute, apply, middle, at):
        compute(0, 0)

        def body(i, carry):
            @pl.when(i == at)
            def _():
                middle()

            compute(2 * i + 1, 1)
            apply(2 * i, 0)
            compute(jnp.minimum(2 * i + 2, count - 1), 0)
            apply(2 * i + 1, 1)
            return carry

        lax.fori_loop(0, count // 2, body, 0)

    def self_middle():
        wait(phase1)
        start(phase2)

    section(CL_DEV, self_compute, self_apply, self_middle, CL_DEV // 4)
    wait(phase2)
    start(phase3)
    wait(heads)
    for j in range(EDGE):
        cw[CL_DEV + j] = split_rows(next_w[:, cluster_cols(j)])
        pos_c[CL_DEV + j, 0:3, :] = next_pos[:, cluster_cols(j)]
    section(PAIRS, pair_compute, pair_apply, lambda: start(give_back), CROSS_DEV // 2)
    wait(phase3)
    wait(give_back)


def far_kernel(
    far_in, proxy_table, basis, weight, self_sum, first_sum, second_sum, returned,
    local_pairs, cross_pairs, cross_count, info_in, out, near,
):
    def strided(j):
        return far_in[pl.ds(j, DEVICES, stride=ROWS), :]

    coef = jnp.concatenate([strided(0), strided(1)], axis=0)
    source = jnp.concatenate([strided(2), strided(3)], axis=0)
    row, lane = iotas((FAR_DEV, 128))
    number = jnp.sum(jnp.where(lane == 3 * RANK, source, 0.0), axis=1, keepdims=True).astype(jnp.int32)
    row, lane = iotas((FAR_DEV, CL_DEV))
    pick = ones_where(lane == number)
    target = sum(dot(pick, part, (1, 0)) for part in split(proxy_table[...], 3))
    row, lane = iotas((128, 3 * 256))
    axis = lane // 256
    from_target = ones_where(row == axis * RANK + lax.rem(lane, 256) // RANK)
    from_source = -ones_where(row == axis * RANK + lax.rem(lane, RANK))
    ends = split(target, 3) + split(source, 3)
    picks = [from_target] * 3 + [from_source] * 3
    offsets = sum(
        dot(jnp.concatenate(ends[i : i + 2], axis=1), jnp.concatenate(picks[i : i + 2], axis=0), (1, 0))
        for i in range(0, 6, 2)
    )
    offsets = offsets * offsets
    coupling = lax.rsqrt(offsets[:, :256] + offsets[:, 256:512] + offsets[:, 512:] + SOFTENING)
    coupling_parts = split(coupling, 2)
    coef_parts = jnp.concatenate(split(coef, 2), axis=1)
    contrib = jnp.zeros((FAR_DEV, 128), F32)
    row, lane = iotas((256, 256))
    half = lane // 128
    place = lax.rem(lane, 128)
    widen_from = row - (place // RHS) * RANK - half
    repeat_from = lax.rem(row, 128) - lax.rem(lane, RHS) - half * RHS
    for l in range(0, RANK, 2):
        widen = ones_where(widen_from == l)
        repeat = ones_where(repeat_from == l * RHS)
        left = dot(coupling_parts[0], widen, (1, 0)) + dot(coupling_parts[1], widen, (1, 0))
        product = left * dot(coef_parts, repeat, (1, 0))
        contrib = contrib + product[:, :128] + product[:, 128:]
    rowcoef = sum(dot(pick, part, (0, 0)) for part in split(contrib, 3))
    row, lane = iotas((CL_DEV * RHS, CL_DEV))
    eight = ones_where(row // RHS == lane)
    wide = sum(dot(eight, part, (1, 0)) for part in split(rowcoef, 3))
    row, lane = iotas(wide.shape)
    wide = jnp.where(lax.rem(row, RHS) == lax.rem(lane, RHS), wide, 0.0)
    row, lane = iotas((128, RANK))
    narrow = ones_where(row // RHS == lane)
    rows = sum(dot(part, narrow, (1, 0)) for part in split(wide, 3))
    rows_high = rows.astype(BF16).astype(F32)
    lefts = jnp.concatenate([rows_high, rows_high, rows - rows_high], axis=1)
    for c in range(CL_DEV):
        block = basis[:, cluster_cols(c)]
        high = block.astype(BF16).astype(F32)
        parts = jnp.concatenate([high, block - high, high], axis=0).astype(BF16)
        near[c] = self_sum[c] + dot(lefts[c * RHS : (c + 1) * RHS].astype(BF16), parts, (1, 0))

    def add_local(t, carry):
        near[local_pairs[0, t]] += first_sum[CROSS_DEV + t]
        near[local_pairs[1, t]] += second_sum[CROSS_DEV + t]
        return carry

    lax.fori_loop(0, LOC_DEV, add_local, 0)

    def add_cross(t, carry):
        near[cross_pairs[0, t]] += first_sum[t]
        return carry

    lax.fori_loop(0, cross_count[0], add_cross, 0)

    def add_returned(t, carry):
        near[info_in[1, t]] += returned[t]
        return carry

    lax.fori_loop(0, info_in[2, 0], add_returned, 0)
    for c in range(CL_DEV):
        cols = cluster_cols(c)
        out[:, cols] = near[c] * (weight[:, cols] * FOUR_PI_INV)


def on_device(
    positions, panel_weight, charges, basis, proxies, local_pairs, cross_pairs, cross_count, far_blocks
):
    panels = positions.shape[1]
    weight = panel_weight.reshape(1, panels)
    vmem = pl.BlockSpec(memory_space=pltpu.VMEM)
    smem = pl.BlockSpec(memory_space=pltpu.SMEM)
    hbm = pl.BlockSpec(memory_space=pltpu.HBM)

    def floats(*shape):
        return pltpu.VMEM(shape, F32)

    outs = pl.pallas_call(
        near_kernel,
        out_shape=[
            jax.ShapeDtypeStruct((CL_DEV, RHS, CLUSTER), F32),
            jax.ShapeDtypeStruct((PAIRS, RHS, CLUSTER), F32),
            jax.ShapeDtypeStruct((PAIRS, RHS, CLUSTER), F32),
            jax.ShapeDtypeStruct((N_ZC, N_X, N_Y, ROWS, 128), F32),
            jax.ShapeDtypeStruct((CROSS_DEV, RHS, CLUSTER), F32),
            jax.ShapeDtypeStruct((8, 128), jnp.int32),
            jax.ShapeDtypeStruct((CL_DEV, 128), F32),
        ],
        in_specs=[hbm] * 4 + [vmem] * 3 + [smem] * 3,
        out_specs=[vmem] * 7,
        scratch_shapes=[
            floats(3, panels),
            floats(1, panels),
            floats(RHS, panels),
            floats(RANK, panels),
            pltpu.VMEM((CL_DEV + EDGE, 2 * RHS, CLUSTER), BF16),
            floats(CL_DEV + EDGE, 8, CLUSTER),
            floats(CL_DEV, CLUSTER, 8),
            floats(CL_DEV * 2 * RANK, 2 * RHS),
            floats(FAR_DEV, 128),
            floats(FAR_DEV, 128),
            floats(DEVICES * ROWS, 128),
            floats(N_Y, N_X * N_ZC * ROWS, 128),
            floats(N_X, N_Y, N_ZC * ROWS, 128),
            floats(RHS, EDGE_PANELS),
            floats(3, EDGE_PANELS),
            floats(RHS, EDGE_PANELS),
            pltpu.VMEM((8, 128), jnp.int32),
        ]
        + [pltpu.VMEM((CLUSTER, CLUSTER), BF16)] * 4
        + [pltpu.SemaphoreType.DMA((count,)) for count in (4, 13, 13, 3, 4, 4)],
        compiler_params=pltpu.CompilerParams(
            collective_id=0, has_side_effects=True, vmem_limit_bytes=30 * 2**20
        ),
    )(
        positions, weight, charges, basis, proxies, far_blocks, cross_pairs, local_pairs, cross_pairs, cross_count
    )
    self_sum, first_sum, second_sum, far_in, returned, info_in, proxy_table = outs
    return pl.pallas_call(
        far_kernel,
        out_shape=jax.ShapeDtypeStruct((RHS, panels), F32),
        in_specs=[vmem] * 8 + [smem] * 4,
        out_specs=vmem,
        scratch_shapes=[floats(CL_DEV, RHS, CLUSTER)],
        compiler_params=pltpu.CompilerParams(vmem_limit_bytes=30 * 2**20),
    )(
        far_in.reshape(-1, 128), proxy_table, basis, weight, self_sum, first_sum, second_sum,
        returned, local_pairs, cross_pairs, cross_count, info_in,
    )


def solution(mesh):
    whole = P(None, ("gx", "gy"))
    flat = P(("gx", "gy"))
    return jax.shard_map(
        on_device,
        mesh=mesh,
        in_specs=(whole, flat, whole, whole, whole, whole, whole, flat, whole),
        out_specs=whole,
        check_vma=False,
    )
```

```python
import functools

import jax
import jax.numpy as jnp
from jax import lax
from jax.experimental import pallas as pl
from jax.experimental.pallas import tpu as pltpu
from jax.sharding import PartitionSpec as P

CLUSTER = 512
RANK = 16
RHS = 8
EDGE = 8
FOUR_PI_INV = 0.07957747154594767
SOFTENING = 0.0025
CL_DEV = 32
LOC_DEV = 32
CROSS_DEV = 16
PAIRS = CROSS_DEV + LOC_DEV
EARLY = 8
FAR_DEV = 256
EDGE_PANELS = EDGE * CLUSTER
CHUNK = 32
STRIP = 128
DEVICES = 128
N_Y, N_X, N_ZC = 4, 4, 8
ROWS = 8
MESH = pl.DeviceIdType.MESH
F32 = jnp.float32
BF16 = jnp.bfloat16


def dot(a, b, dims):
    return lax.dot_general(a, b, ((dims[:1], dims[1:]), ((), ())), preferred_element_type=F32)


def split(value, parts):
    out = []
    for _ in range(parts - 1):
        high = value.astype(BF16)
        out.append(high)
        value = value - high.astype(F32)
    out.append(value.astype(BF16))
    return out


def split_rows(value):
    high = value.astype(BF16).astype(F32)
    return jnp.concatenate([high, value - high], axis=0).astype(BF16)


def iotas(shape):
    return lax.broadcasted_iota(jnp.int32, shape, 0), lax.broadcasted_iota(jnp.int32, shape, 1)


def ones_where(condition):
    return jnp.where(condition, 1.0, 0.0).astype(BF16)


def cluster_cols(c):
    return slice(c * CLUSTER, (c + 1) * CLUSTER)


def near_kernel(
    pos_hbm, weight_hbm, charges_hbm, basis_hbm, proxies, far_blocks, cross_vector, local_pairs, cross_pairs, cross_count,
    self_out, first_out, second_out, far_in, returned, info_in, proxy_table,
    self_sum, first_sum, second_sum, pos, weight, charges, basis, cw, pos_c, pos_t, moments, coef_rows, proxy_rows, send, recv1, recv2, head_w, next_pos, next_w,
    info, hi0, hi1, lo0, lo1, load_sem, far_send, far_recv, far_own, edge_send, edge_recv, out_sem,
):
    y = lax.axis_index("gx")
    gy = lax.axis_index("gy")
    x = gy // N_ZC
    zc = lax.rem(gy, N_ZC)
    flat = y * (N_X * N_ZC) + gy
    tile_hi, tile_lo = (hi0, hi1), (lo0, lo1)

    loads = [
        pltpu.make_async_copy(source, target, load_sem.at[i])
        for i, (source, target) in enumerate(
            ((weight_hbm, weight), (charges_hbm, charges), (pos_hbm, pos), (basis_hbm, basis))
        )
    ]
    for load in loads:
        load.start()

    def device_of(index):
        return (index // (N_X * N_ZC), lax.rem(index, N_X * N_ZC))

    after = device_of(lax.rem(flat + 1, DEVICES))
    before = device_of(lax.rem(flat + DEVICES - 1, DEVICES))
    peers = (
        [(lax.rem(y + i, N_Y), gy) for i in range(1, N_Y)]
        + [(y, lax.rem(x + i, N_X) * N_ZC + zc) for i in range(1, N_X)]
        + [(y, x * N_ZC + lax.rem(zc + i, N_ZC)) for i in range(1, N_ZC)]
    )
    barrier = pltpu.get_barrier_semaphore()
    for peer in peers + [after, before]:
        pl.semaphore_signal(barrier, inc=1, device_id=peer, device_id_type=MESH)

    info[...] = jnp.zeros_like(info)
    info[0:2, 0:CROSS_DEV] = cross_vector[...]
    info[2:3, :] = jnp.full((1, 128), cross_count[0], jnp.int32)

    columns = jnp.concatenate([proxies[...], jnp.zeros((5, CL_DEV * RANK), F32)], axis=0).T
    row, lane = iotas((CL_DEV * RANK, 128))
    spread = jnp.where(
        lane < RANK, columns[:, 0:1], jnp.where(lane < 2 * RANK, columns[:, 1:2], columns[:, 2:3])
    )
    spread = jnp.where((lax.rem(row, RANK) == lax.rem(lane, RANK)) & (lane < 3 * RANK), spread, 0.0)
    row, lane = iotas((CL_DEV, CL_DEV * RANK))
    gather = ones_where(row == lane // RANK)
    table = sum(dot(gather, part, (1, 0)) for part in split(spread, 3))
    proxy_table[...] = table

    for load in loads:
        load.wait()
    for c in range(CL_DEV):
        cols = cluster_cols(c)
        parts = split_rows(charges[:, cols] * weight[:, cols])
        cw[c] = parts
        place = jnp.concatenate([pos[:, cols], jnp.zeros((5, CLUSTER), F32)], axis=0)
        pos_c[c] = place
        pos_t[c] = place.T
        moments[c * 32 : (c + 1) * 32, :] = dot(split_rows(basis[:, cols]), parts, (1, 1))
    head_w[...] = charges[:, :EDGE_PANELS] * weight[:, :EDGE_PANELS]

    row, lane = iotas((2 * RHS, 128))
    spread = ones_where(lax.rem(row, RHS) == lax.rem(lane, RHS))
    wide = sum(dot(part, spread, (1, 0)) for part in split(moments[...], 3))
    row, lane = iotas(wide.shape)
    wide = jnp.where(lax.rem(row, RANK) == lane // RHS, wide, 0.0)
    coef = jnp.sum(wide.reshape(CL_DEV, 2 * RANK, 128), axis=1)

    row, lane = iotas((CL_DEV, 256))
    numbers = jnp.where(lane == 128 + 3 * RANK, row.astype(F32), 0.0).astype(BF16)
    both = jnp.concatenate(split(jnp.concatenate([coef, table], axis=1), 3) + [numbers], axis=0)
    row, lane = iotas((3 * CL_DEV, FAR_DEV))
    pick_source = jnp.where(lax.rem(row, CL_DEV) == far_blocks[0:1, :], 1.0, 0.0)
    row, lane = iotas((CL_DEV, FAR_DEV))
    pick_number = jnp.where(row == (far_blocks[1:2, :] & (CL_DEV - 1)), 1.0, 0.0)
    pick = jnp.concatenate([pick_source, pick_number], axis=0).astype(BF16)
    picked = dot(pick, both, (0, 0))
    coef_rows[...] = picked[:, :128]
    proxy_rows[...] = picked[:, 128:]
    for j in range(2):
        send[pl.ds(j, DEVICES, stride=ROWS), :] = coef_rows[pl.ds(j, DEVICES, stride=2), :]
        for k in range(2, ROWS, 2):
            send[pl.ds(k + j, DEVICES, stride=ROWS), :] = proxy_rows[pl.ds(j, DEVICES, stride=2), :]

    def far_copy(source, target, index, peer):
        return pltpu.make_async_remote_copy(
            src_ref=source, dst_ref=target, send_sem=far_send.at[index], recv_sem=far_recv.at[index],
            device_id=peer, device_id_type=MESH,
        )

    def edge_copy(source, target, index, peer):
        return pltpu.make_async_remote_copy(
            src_ref=source, dst_ref=target, send_sem=edge_send.at[index], recv_sem=edge_recv.at[index],
            device_id=peer, device_id_type=MESH,
        )

    def start(copies):
        for copy in copies:
            copy.start()

    def wait(copies):
        for copy in copies:
            copy.wait()

    def part(index, count):
        return pl.ds(pl.multiple_of(index * count, count), count)

    per_y, per_x = N_X * N_ZC * ROWS, N_ZC * ROWS
    phase1 = [pltpu.make_async_copy(send.at[part(y, per_y)], recv1.at[0], far_own.at[0])] + [
        far_copy(send.at[part(lax.rem(y + i, N_Y), per_y)], recv1.at[i], i - 1, peers[i - 1])
        for i in range(1, N_Y)
    ]
    phase2 = [pltpu.make_async_copy(recv1.at[:, part(x, per_x)], recv2.at[0], far_own.at[1])] + [
        far_copy(recv1.at[:, part(lax.rem(x + i, N_X), per_x)], recv2.at[i], 2 + i, peers[2 + i])
        for i in range(1, N_X)
    ]
    phase3 = [pltpu.make_async_copy(recv2.at[:, :, part(zc, ROWS)], far_in.at[0], far_own.at[2])] + [
        far_copy(recv2.at[:, :, part(lax.rem(zc + i, N_ZC), ROWS)], far_in.at[i], 5 + i, peers[5 + i])
        for i in range(1, N_ZC)
    ]
    heads = [
        edge_copy(pos.at[:, pl.ds(0, EDGE_PANELS)], next_pos, 0, before),
        edge_copy(head_w, next_w, 1, before),
        edge_copy(info, info_in, 2, after),
    ]
    crossing = pl.ds(EARLY, CROSS_DEV)
    give_back = [edge_copy(second_sum.at[crossing], returned, 3, after)]

    def out_copies(index, first, count, *pairs):
        rows = pl.ds(first, count)
        return [
            pltpu.make_async_copy(source.at[rows], target.at[rows], out_sem.at[index + i])
            for i, (source, target) in enumerate(pairs)
        ]

    first_pair, second_pair = (first_sum, first_out), (second_sum, second_out)
    done = EARLY + CROSS_DEV
    outs_self = out_copies(0, 0, CL_DEV, (self_sum, self_out))
    outs_early = out_copies(1, 0, done, first_pair) + out_copies(2, 0, EARLY, second_pair)
    outs_late = out_copies(3, done, 16, first_pair, second_pair)
    outs_last = out_copies(5, done + 16, 8, first_pair, second_pair)

    def fill(row_cluster, columns, slot, row_from, row_to, col_from):
        col_x = columns[0:1, col_from:]
        col_y = columns[1:2, col_from:]
        col_z = columns[2:3, col_from:]
        for begin in range(row_from, row_to, CHUNK):
            rows = pos_t[row_cluster, begin : begin + CHUNK, :]
            dx = rows[:, 0:1] - col_x
            dy = rows[:, 1:2] - col_y
            dz = rows[:, 2:3] - col_z
            value = lax.rsqrt(dx * dx + dy * dy + dz * dz + SOFTENING)
            high = value.astype(BF16)
            tile_hi[slot][begin : begin + CHUNK, col_from:] = high
            tile_lo[slot][begin : begin + CHUNK, col_from:] = (value - high.astype(F32)).astype(BF16)

    def halves(parts, slot, rows, cols, side):
        sums = dot(parts, tile_hi[slot][rows, cols], (1, side)) + dot(parts, tile_lo[slot][rows, cols], (1, side))
        return sums[:RHS] + sums[RHS:]

    whole = slice(0, CLUSTER)

    def self_compute(t, slot):
        columns = pos_c[t]
        for begin in range(0, CLUSTER, STRIP):
            fill(t, columns, slot, begin, begin + STRIP, begin)

    def self_apply(t, slot):
        parts = cw[t]
        sums = [None] * (CLUSTER // STRIP)
        for i in range(CLUSTER // STRIP):
            rows = slice(i * STRIP, (i + 1) * STRIP)
            down = halves(parts[:, rows], slot, rows, slice(i * STRIP, CLUSTER), 0)
            for j in range(i, CLUSTER // STRIP):
                piece = down[:, (j - i) * STRIP : (j - i + 1) * STRIP]
                sums[j] = piece if sums[j] is None else sums[j] + piece
            if i + 1 < CLUSTER // STRIP:
                rest = slice((i + 1) * STRIP, CLUSTER)
                sums[i] = sums[i] + halves(parts[:, rest], slot, rows, rest, 1)
        self_sum[t] = jnp.concatenate(sums, axis=1)

    def pair_of(t):
        crosses = (t >= EARLY) & (t < done)
        c = jnp.clip(t - EARLY, 0, CROSS_DEV - 1)
        l = jnp.clip(jnp.where(t < EARLY, t, t - CROSS_DEV), 0, LOC_DEV - 1)
        first = jnp.where(crosses, cross_pairs[0, c], local_pairs[0, l])
        second = jnp.where(crosses, cross_pairs[1, c] + CL_DEV, local_pairs[1, l])
        return first, second

    def pair_compute(t, slot):
        first, second = pair_of(t)
        fill(first, pos_c[second], slot, 0, CLUSTER, 0)

    def pair_apply(t, slot):
        first, second = pair_of(t)
        first_sum[t] = halves(cw[second], slot, whole, whole, 1)
        second_sum[t] = halves(cw[first], slot, whole, whole, 0)

    def section(count, compute, apply, steps):
        compute(0, 0)

        def body(i, carry):
            for at, step in steps:
                pl.when(i == at)(step)
            compute(2 * i + 1, 1)
            apply(2 * i, 0)
            compute(jnp.minimum(2 * i + 2, count - 1), 0)
            apply(2 * i + 1, 1)
            return carry

        lax.fori_loop(0, count // 2, body, 0)

    def send_first():
        pl.semaphore_wait(barrier, len(peers) + 2)
        start(heads)
        start(phase1)

    def take_heads():
        wait(heads)
        for j in range(EDGE):
            cw[CL_DEV + j] = split_rows(next_w[:, cluster_cols(j)])
            pos_c[CL_DEV + j, 0:3, :] = next_pos[:, cluster_cols(j)]

    def send_last():
        wait(phase2)
        start(phase3)

    def send_back():
        start(give_back)
        start(outs_early)

    section(CL_DEV, self_compute, self_apply, [(2, send_first)])
    start(outs_self)
    wait(phase1)
    start(phase2)
    section(
        PAIRS,
        pair_compute,
        pair_apply,
        [(EARLY // 2 - 1, take_heads), (10, send_last), (done // 2, send_back), (done // 2 + 8, lambda: start(outs_late))],
    )
    start(outs_last)
    wait(outs_self)
    wait(outs_early)
    wait(outs_late)
    wait(phase3)
    wait(give_back)
    wait(outs_last)


def far_kernel(
    far_hbm, proxy_table, basis_hbm, weight_hbm, self_hbm, first_hbm, second_hbm, returned_hbm,
    local_pairs, cross_pairs, cross_count, info_in,
    out, near, far_in, basis, weight, self_sum, first_sum, second_sum, returned, load_sem,
):
    loads = [
        pltpu.make_async_copy(source, target, load_sem.at[i])
        for i, (source, target) in enumerate(
            (
                (far_hbm, far_in),
                (basis_hbm, basis),
                (self_hbm, self_sum),
                (first_hbm, first_sum),
                (second_hbm, second_sum),
                (returned_hbm, returned),
                (weight_hbm, weight),
            )
        )
    ]
    for load in loads:
        load.start()
    loads[0].wait()

    def strided(j):
        return far_in[pl.ds(j, DEVICES, stride=ROWS), :]

    coef = jnp.concatenate([strided(0), strided(1)], axis=0)
    source = jnp.concatenate([strided(2), strided(3)], axis=0)
    row, lane = iotas((FAR_DEV, 128))
    number = jnp.sum(jnp.where(lane == 3 * RANK, source, 0.0), axis=1, keepdims=True).astype(jnp.int32)
    row, lane = iotas((FAR_DEV, CL_DEV))
    pick = ones_where(lane == number)
    target = sum(dot(pick, part, (1, 0)) for part in split(proxy_table[...], 3))
    row, lane = iotas((128, 3 * 256))
    axis = lane // 256
    from_target = ones_where(row == axis * RANK + lax.rem(lane, 256) // RANK)
    from_source = -ones_where(row == axis * RANK + lax.rem(lane, RANK))
    ends = split(target, 3) + split(source, 3)
    picks = [from_target] * 3 + [from_source] * 3
    offsets = sum(
        dot(jnp.concatenate(ends[i : i + 2], axis=1), jnp.concatenate(picks[i : i + 2], axis=0), (1, 0))
        for i in range(0, 6, 2)
    )
    offsets = offsets * offsets
    coupling = lax.rsqrt(offsets[:, :256] + offsets[:, 256:512] + offsets[:, 512:] + SOFTENING)
    coupling_parts = split(coupling, 2)
    coef_parts = jnp.concatenate(split(coef, 2), axis=1)
    contrib = jnp.zeros((FAR_DEV, 128), F32)
    row, lane = iotas((256, 256))
    half = lane // 128
    place = lax.rem(lane, 128)
    widen_from = row - (place // RHS) * RANK - half
    repeat_from = lax.rem(row, 128) - lax.rem(lane, RHS) - half * RHS
    for l in range(0, RANK, 2):
        widen = ones_where(widen_from == l)
        repeat = ones_where(repeat_from == l * RHS)
        left = dot(coupling_parts[0], widen, (1, 0)) + dot(coupling_parts[1], widen, (1, 0))
        product = left * dot(coef_parts, repeat, (1, 0))
        contrib = contrib + product[:, :128] + product[:, 128:]
    rowcoef = sum(dot(pick, part, (0, 0)) for part in split(contrib, 3))
    row, lane = iotas((CL_DEV * RHS, CL_DEV))
    eight = ones_where(row // RHS == lane)
    wide = sum(dot(eight, part, (1, 0)) for part in split(rowcoef, 3))
    row, lane = iotas(wide.shape)
    wide = jnp.where(lax.rem(row, RHS) == lax.rem(lane, RHS), wide, 0.0)
    row, lane = iotas((128, RANK))
    narrow = ones_where(row // RHS == lane)
    rows = sum(dot(part, narrow, (1, 0)) for part in split(wide, 3))
    rows_high = rows.astype(BF16).astype(F32)
    lefts = jnp.concatenate([rows_high, rows_high, rows - rows_high], axis=1)
    for load in loads[1:]:
        load.wait()
    for c in range(CL_DEV):
        block = basis[:, cluster_cols(c)]
        high = block.astype(BF16).astype(F32)
        parts = jnp.concatenate([high, block - high, high], axis=0).astype(BF16)
        near[c] = self_sum[c] + dot(lefts[c * RHS : (c + 1) * RHS].astype(BF16), parts, (1, 0))

    def add_local(t, carry):
        slot = jnp.where(t < EARLY, t, t + CROSS_DEV)
        near[local_pairs[0, t]] += first_sum[slot]
        near[local_pairs[1, t]] += second_sum[slot]
        return carry

    lax.fori_loop(0, LOC_DEV, add_local, 0)

    def add_cross(t, carry):
        near[cross_pairs[0, t]] += first_sum[EARLY + t]
        return carry

    lax.fori_loop(0, cross_count[0], add_cross, 0)

    def add_returned(t, carry):
        near[info_in[1, t]] += returned[t]
        return carry

    lax.fori_loop(0, info_in[2, 0], add_returned, 0)
    for c in range(CL_DEV):
        cols = cluster_cols(c)
        out[:, cols] = near[c] * (weight[:, cols] * FOUR_PI_INV)


def on_device(
    positions, panel_weight, charges, basis, proxies, local_pairs, cross_pairs, cross_count, far_blocks
):
    panels = positions.shape[1]
    weight = panel_weight.reshape(1, panels)
    vmem = pl.BlockSpec(memory_space=pltpu.VMEM)
    smem = pl.BlockSpec(memory_space=pltpu.SMEM)
    hbm = pl.BlockSpec(memory_space=pltpu.HBM)

    def floats(*shape):
        return pltpu.VMEM(shape, F32)

    outs = pl.pallas_call(
        near_kernel,
        out_shape=[
            jax.ShapeDtypeStruct((CL_DEV, RHS, CLUSTER), F32),
            jax.ShapeDtypeStruct((PAIRS, RHS, CLUSTER), F32),
            jax.ShapeDtypeStruct((PAIRS, RHS, CLUSTER), F32),
            jax.ShapeDtypeStruct((N_ZC, N_X, N_Y, ROWS, 128), F32),
            jax.ShapeDtypeStruct((CROSS_DEV, RHS, CLUSTER), F32),
            jax.ShapeDtypeStruct((8, 128), jnp.int32),
            jax.ShapeDtypeStruct((CL_DEV, 128), F32),
        ],
        in_specs=[hbm] * 4 + [vmem] * 3 + [smem] * 3,
        out_specs=[hbm] * 6 + [vmem],
        scratch_shapes=[
            floats(CL_DEV, RHS, CLUSTER),
            floats(PAIRS, RHS, CLUSTER),
            floats(PAIRS, RHS, CLUSTER),
            floats(3, panels),
            floats(1, panels),
            floats(RHS, panels),
            floats(RANK, panels),
            pltpu.VMEM((CL_DEV + EDGE, 2 * RHS, CLUSTER), BF16),
            floats(CL_DEV + EDGE, 8, CLUSTER),
            floats(CL_DEV, CLUSTER, 8),
            floats(CL_DEV * 2 * RANK, 2 * RHS),
            floats(FAR_DEV, 128),
            floats(FAR_DEV, 128),
            floats(DEVICES * ROWS, 128),
            floats(N_Y, N_X * N_ZC * ROWS, 128),
            floats(N_X, N_Y, N_ZC * ROWS, 128),
            floats(RHS, EDGE_PANELS),
            floats(3, EDGE_PANELS),
            floats(RHS, EDGE_PANELS),
            pltpu.VMEM((8, 128), jnp.int32),
        ]
        + [pltpu.VMEM((CLUSTER, CLUSTER), BF16)] * 4
        + [pltpu.SemaphoreType.DMA((count,)) for count in (4, 13, 13, 3, 4, 4, 7)],
        compiler_params=pltpu.CompilerParams(
            collective_id=0, has_side_effects=True, vmem_limit_bytes=60 * 2**20
        ),
    )(
        positions, weight, charges, basis, proxies, far_blocks, cross_pairs, local_pairs, cross_pairs, cross_count
    )
    self_sum, first_sum, second_sum, far_in, returned, info_in, proxy_table = outs
    return pl.pallas_call(
        far_kernel,
        out_shape=jax.ShapeDtypeStruct((RHS, panels), F32),
        in_specs=[hbm, vmem] + [hbm] * 6 + [smem] * 4,
        out_specs=vmem,
        scratch_shapes=[
            floats(CL_DEV, RHS, CLUSTER),
            floats(DEVICES * ROWS, 128),
            floats(RANK, panels),
            floats(1, panels),
            floats(CL_DEV, RHS, CLUSTER),
            floats(PAIRS, RHS, CLUSTER),
            floats(PAIRS, RHS, CLUSTER),
            floats(CROSS_DEV, RHS, CLUSTER),
            pltpu.SemaphoreType.DMA((7,)),
        ],
        compiler_params=pltpu.CompilerParams(vmem_limit_bytes=60 * 2**20),
    )(
        far_in.reshape(-1, 128), proxy_table, basis, weight, self_sum, first_sum, second_sum,
        returned, local_pairs, cross_pairs, cross_count, info_in,
    )


def solution(mesh):
    whole = P(None, ("gx", "gy"))
    flat = P(("gx", "gy"))
    return jax.shard_map(
        on_device,
        mesh=mesh,
        in_specs=(whole, flat, whole, whole, whole, whole, whole, flat, whole),
        out_specs=whole,
        check_vma=False,
    )
```

```python
import functools

import jax
import jax.numpy as jnp
from jax import lax
from jax.experimental import pallas as pl
from jax.experimental.pallas import tpu as pltpu
from jax.sharding import PartitionSpec as P

CLUSTER = 512
RANK = 16
RHS = 8
EDGE = 8
FOUR_PI_INV = 0.07957747154594767
SOFTENING = 0.0025
CL_DEV = 32
LOC_DEV = 32
CROSS_DEV = 16
PAIRS = CROSS_DEV + LOC_DEV
EARLY = 8
FAR_DEV = 256
EDGE_PANELS = EDGE * CLUSTER
SELF_CHUNK = 32
PAIR_CHUNK = 16
STRIP = 128
DEVICES = 128
N_Y, N_X, N_ZC = 4, 4, 8
ROWS = 8
MESH = pl.DeviceIdType.MESH
F32 = jnp.float32
BF16 = jnp.bfloat16


def dot(a, b, dims):
    return lax.dot_general(a, b, ((dims[:1], dims[1:]), ((), ())), preferred_element_type=F32)


def split(value, parts):
    out = []
    for _ in range(parts - 1):
        high = value.astype(BF16)
        out.append(high)
        value = value - high.astype(F32)
    out.append(value.astype(BF16))
    return out


def split_rows(value):
    high = value.astype(BF16).astype(F32)
    return jnp.concatenate([high, value - high], axis=0).astype(BF16)


def iotas(shape):
    return lax.broadcasted_iota(jnp.int32, shape, 0), lax.broadcasted_iota(jnp.int32, shape, 1)


def ones_where(condition):
    return jnp.where(condition, 1.0, 0.0).astype(BF16)


def cluster_cols(c):
    return slice(c * CLUSTER, (c + 1) * CLUSTER)


def near_kernel(
    pos_hbm, weight_hbm, charges_hbm, basis_hbm, proxies, far_blocks, cross_vector, local_pairs, cross_pairs, cross_count,
    self_out, first_out, second_out, far_in, returned, info_in, proxy_table,
    self_sum, first_sum, second_sum, pos, weight, charges, basis, cw, pos_c, pos_t, moments, coef_rows, proxy_rows, send, recv1, recv2, head_w, next_pos, next_w,
    info, hi0, hi1, lo0, lo1, load_sem, far_send, far_recv, far_own, edge_send, edge_recv, out_sem,
):
    y = lax.axis_index("gx")
    gy = lax.axis_index("gy")
    x = gy // N_ZC
    zc = lax.rem(gy, N_ZC)
    flat = y * (N_X * N_ZC) + gy
    tile_hi, tile_lo = (hi0, hi1), (lo0, lo1)

    loads = [
        pltpu.make_async_copy(source, target, load_sem.at[i])
        for i, (source, target) in enumerate(
            ((weight_hbm, weight), (charges_hbm, charges), (pos_hbm, pos), (basis_hbm, basis))
        )
    ]
    for load in loads:
        load.start()

    def device_of(index):
        return (index // (N_X * N_ZC), lax.rem(index, N_X * N_ZC))

    after = device_of(lax.rem(flat + 1, DEVICES))
    before = device_of(lax.rem(flat + DEVICES - 1, DEVICES))
    peers = (
        [(lax.rem(y + i, N_Y), gy) for i in range(1, N_Y)]
        + [(y, lax.rem(x + i, N_X) * N_ZC + zc) for i in range(1, N_X)]
        + [(y, x * N_ZC + lax.rem(zc + i, N_ZC)) for i in range(1, N_ZC)]
    )
    barrier = pltpu.get_barrier_semaphore()
    for peer in peers + [after, before]:
        pl.semaphore_signal(barrier, inc=1, device_id=peer, device_id_type=MESH)

    info[...] = jnp.zeros_like(info)
    info[0:2, 0:CROSS_DEV] = cross_vector[...]
    info[2:3, :] = jnp.full((1, 128), cross_count[0], jnp.int32)

    columns = jnp.concatenate([proxies[...], jnp.zeros((5, CL_DEV * RANK), F32)], axis=0).T
    row, lane = iotas((CL_DEV * RANK, 128))
    spread = jnp.where(
        lane < RANK, columns[:, 0:1], jnp.where(lane < 2 * RANK, columns[:, 1:2], columns[:, 2:3])
    )
    spread = jnp.where((lax.rem(row, RANK) == lax.rem(lane, RANK)) & (lane < 3 * RANK), spread, 0.0)
    row, lane = iotas((CL_DEV, CL_DEV * RANK))
    gather = ones_where(row == lane // RANK)
    table = sum(dot(gather, part, (1, 0)) for part in split(spread, 3))
    proxy_table[...] = table

    for load in loads:
        load.wait()
    for c in range(CL_DEV):
        cols = cluster_cols(c)
        parts = split_rows(charges[:, cols] * weight[:, cols])
        cw[c] = parts
        place = jnp.concatenate([pos[:, cols], jnp.zeros((5, CLUSTER), F32)], axis=0)
        pos_c[c] = place
        pos_t[c] = place.T
        moments[c * 32 : (c + 1) * 32, :] = dot(split_rows(basis[:, cols]), parts, (1, 1))
    head_w[...] = charges[:, :EDGE_PANELS] * weight[:, :EDGE_PANELS]

    row, lane = iotas((2 * RHS, 128))
    spread = ones_where(lax.rem(row, RHS) == lax.rem(lane, RHS))
    wide = sum(dot(part, spread, (1, 0)) for part in split(moments[...], 3))
    row, lane = iotas(wide.shape)
    wide = jnp.where(lax.rem(row, RANK) == lane // RHS, wide, 0.0)
    coef = jnp.sum(wide.reshape(CL_DEV, 2 * RANK, 128), axis=1)

    row, lane = iotas((CL_DEV, 256))
    numbers = jnp.where(lane == 128 + 3 * RANK, row.astype(F32), 0.0).astype(BF16)
    both = jnp.concatenate(split(jnp.concatenate([coef, table], axis=1), 3) + [numbers], axis=0)
    row, lane = iotas((3 * CL_DEV, FAR_DEV))
    pick_source = jnp.where(lax.rem(row, CL_DEV) == far_blocks[0:1, :], 1.0, 0.0)
    row, lane = iotas((CL_DEV, FAR_DEV))
    pick_number = jnp.where(row == (far_blocks[1:2, :] & (CL_DEV - 1)), 1.0, 0.0)
    pick = jnp.concatenate([pick_source, pick_number], axis=0).astype(BF16)
    picked = dot(pick, both, (0, 0))
    coef_rows[...] = picked[:, :128]
    proxy_rows[...] = picked[:, 128:]
    for j in range(2):
        send[pl.ds(j, DEVICES, stride=ROWS), :] = coef_rows[pl.ds(j, DEVICES, stride=2), :]
        for k in range(2, ROWS, 2):
            send[pl.ds(k + j, DEVICES, stride=ROWS), :] = proxy_rows[pl.ds(j, DEVICES, stride=2), :]

    def far_copy(source, target, index, peer):
        return pltpu.make_async_remote_copy(
            src_ref=source, dst_ref=target, send_sem=far_send.at[index], recv_sem=far_recv.at[index],
            device_id=peer, device_id_type=MESH,
        )

    def edge_copy(source, target, index, peer):
        return pltpu.make_async_remote_copy(
            src_ref=source, dst_ref=target, send_sem=edge_send.at[index], recv_sem=edge_recv.at[index],
            device_id=peer, device_id_type=MESH,
        )

    def start(copies):
        for copy in copies:
            copy.start()

    def wait(copies):
        for copy in copies:
            copy.wait()

    def part(index, count):
        return pl.ds(pl.multiple_of(index * count, count), count)

    per_y, per_x = N_X * N_ZC * ROWS, N_ZC * ROWS
    phase1 = [pltpu.make_async_copy(send.at[part(y, per_y)], recv1.at[0], far_own.at[0])] + [
        far_copy(send.at[part(lax.rem(y + i, N_Y), per_y)], recv1.at[i], i - 1, peers[i - 1])
        for i in range(1, N_Y)
    ]
    phase2 = [pltpu.make_async_copy(recv1.at[:, part(x, per_x)], recv2.at[0], far_own.at[1])] + [
        far_copy(recv1.at[:, part(lax.rem(x + i, N_X), per_x)], recv2.at[i], 2 + i, peers[2 + i])
        for i in range(1, N_X)
    ]
    phase3 = [pltpu.make_async_copy(recv2.at[:, :, part(zc, ROWS)], far_in.at[0], far_own.at[2])] + [
        far_copy(recv2.at[:, :, part(lax.rem(zc + i, N_ZC), ROWS)], far_in.at[i], 5 + i, peers[5 + i])
        for i in range(1, N_ZC)
    ]
    heads = [
        edge_copy(pos.at[:, pl.ds(0, EDGE_PANELS)], next_pos, 0, before),
        edge_copy(head_w, next_w, 1, before),
        edge_copy(info, info_in, 2, after),
    ]
    crossing = pl.ds(EARLY, CROSS_DEV)
    give_back = [edge_copy(second_sum.at[crossing], returned, 3, after)]

    def out_copies(index, first, count, *pairs):
        rows = pl.ds(first, count)
        return [
            pltpu.make_async_copy(source.at[rows], target.at[rows], out_sem.at[index + i])
            for i, (source, target) in enumerate(pairs)
        ]

    first_pair, second_pair = (first_sum, first_out), (second_sum, second_out)
    done = EARLY + CROSS_DEV
    outs_self = out_copies(0, 0, CL_DEV, (self_sum, self_out))
    outs_early = out_copies(1, 0, done, first_pair) + out_copies(2, 0, EARLY, second_pair)
    outs_late = out_copies(3, done, 16, first_pair, second_pair)
    outs_last = out_copies(5, done + 16, 8, first_pair, second_pair)

    def fill(row_cluster, columns, slot, row_from, row_to, col_from, chunk):
        col_x = columns[0:1, col_from:]
        col_y = columns[1:2, col_from:]
        col_z = columns[2:3, col_from:]
        for begin in range(row_from, row_to, chunk):
            rows = pos_t[row_cluster, begin : begin + chunk, :]
            dx = rows[:, 0:1] - col_x
            dy = rows[:, 1:2] - col_y
            dz = rows[:, 2:3] - col_z
            value = lax.rsqrt(dx * dx + dy * dy + dz * dz + SOFTENING)
            high = value.astype(BF16)
            tile_hi[slot][begin : begin + chunk, col_from:] = high
            tile_lo[slot][begin : begin + chunk, col_from:] = (value - high.astype(F32)).astype(BF16)

    def halves(parts, slot, rows, cols, side):
        sums = dot(parts, tile_hi[slot][rows, cols], (1, side)) + dot(parts, tile_lo[slot][rows, cols], (1, side))
        return sums[:RHS] + sums[RHS:]

    whole = slice(0, CLUSTER)

    def self_compute(t, slot):
        columns = pos_c[t]
        for begin in range(0, CLUSTER, STRIP):
            fill(t, columns, slot, begin, begin + STRIP, begin, SELF_CHUNK)

    def self_apply(t, slot):
        parts = cw[t]
        sums = [None] * (CLUSTER // STRIP)
        for i in range(CLUSTER // STRIP):
            rows = slice(i * STRIP, (i + 1) * STRIP)
            down = halves(parts[:, rows], slot, rows, slice(i * STRIP, CLUSTER), 0)
            for j in range(i, CLUSTER // STRIP):
                piece = down[:, (j - i) * STRIP : (j - i + 1) * STRIP]
                sums[j] = piece if sums[j] is None else sums[j] + piece
            if i + 1 < CLUSTER // STRIP:
                rest = slice((i + 1) * STRIP, CLUSTER)
                sums[i] = sums[i] + halves(parts[:, rest], slot, rows, rest, 1)
        self_sum[t] = jnp.concatenate(sums, axis=1)

    def pair_of(t):
        crosses = (t >= EARLY) & (t < done)
        c = jnp.clip(t - EARLY, 0, CROSS_DEV - 1)
        l = jnp.clip(jnp.where(t < EARLY, t, t - CROSS_DEV), 0, LOC_DEV - 1)
        first = jnp.where(crosses, cross_pairs[0, c], local_pairs[0, l])
        second = jnp.where(crosses, cross_pairs[1, c] + CL_DEV, local_pairs[1, l])
        return first, second

    def pair_compute(t, slot):
        first, second = pair_of(t)
        fill(first, pos_c[second], slot, 0, CLUSTER, 0, PAIR_CHUNK)

    def pair_apply(t, slot):
        first, second = pair_of(t)
        first_sum[t] = halves(cw[second], slot, whole, whole, 1)
        second_sum[t] = halves(cw[first], slot, whole, whole, 0)

    def section(count, compute, apply, steps):
        compute(0, 0)

        def body(i, carry):
            for at, step in steps:
                pl.when(i == at)(step)
            compute(2 * i + 1, 1)
            apply(2 * i, 0)
            compute(jnp.minimum(2 * i + 2, count - 1), 0)
            apply(2 * i + 1, 1)
            return carry

        lax.fori_loop(0, count // 2, body, 0)

    def send_first():
        pl.semaphore_wait(barrier, len(peers) + 2)
        start(heads)
        start(phase1)

    def take_heads():
        wait(heads)
        for j in range(EDGE):
            cw[CL_DEV + j] = split_rows(next_w[:, cluster_cols(j)])
            pos_c[CL_DEV + j, 0:3, :] = next_pos[:, cluster_cols(j)]

    def send_last():
        wait(phase2)
        start(phase3)

    def send_back():
        start(give_back)
        start(outs_early)

    section(CL_DEV, self_compute, self_apply, [(2, send_first)])
    start(outs_self)
    wait(phase1)
    start(phase2)
    section(
        PAIRS,
        pair_compute,
        pair_apply,
        [(EARLY // 2 - 1, take_heads), (10, send_last), (done // 2, send_back), (done // 2 + 8, lambda: start(outs_late))],
    )
    start(outs_last)
    wait(outs_self)
    wait(outs_early)
    wait(outs_late)
    wait(phase3)
    wait(give_back)
    wait(outs_last)


def far_kernel(
    far_hbm, proxy_table, basis_hbm, weight_hbm, self_hbm, first_hbm, second_hbm, returned_hbm,
    local_pairs, cross_pairs, cross_count, info_in,
    out, near, far_in, basis, weight, self_sum, first_sum, second_sum, returned, coef, target, coupling, contrib, load_sem,
):
    loads = [
        pltpu.make_async_copy(source, target, load_sem.at[i])
        for i, (source, target) in enumerate(
            (
                (far_hbm, far_in),
                (basis_hbm, basis),
                (self_hbm, self_sum),
                (first_hbm, first_sum),
                (second_hbm, second_sum),
                (returned_hbm, returned),
                (weight_hbm, weight),
            )
        )
    ]
    for load in loads:
        load.start()
    loads[0].wait()

    def strided(j):
        return far_in[pl.ds(j, DEVICES, stride=ROWS), :]

    coef[...] = jnp.concatenate([strided(0).T, strided(1).T], axis=1)
    source = jnp.concatenate([strided(2).T, strided(3).T], axis=1)
    number = source[3 * RANK : 3 * RANK + 1, :].astype(jnp.int32)
    row, lane = iotas((CL_DEV, FAR_DEV))
    pick = ones_where(row == number)
    target[...] = sum(dot(part, pick, (0, 0)) for part in split(proxy_table[...], 3))
    for k in range(RANK):
        distance = SOFTENING
        for axis in range(3):
            end = axis * RANK + k
            offset = target[end : end + 1, :] - source[axis * RANK : (axis + 1) * RANK, :]
            distance = distance + offset * offset
        coupling[k * RANK : (k + 1) * RANK, :] = lax.rsqrt(distance)
    for k in range(RANK):
        total = None
        for l in range(RANK):
            entry = k * RANK + l
            term = coupling[entry : entry + 1, :] * coef[l * RHS : (l + 1) * RHS, :]
            total = term if total is None else total + term
        contrib[k * RHS : (k + 1) * RHS, :] = total
    rowcoef = sum(dot(pick, part, (1, 1)) for part in split(contrib[...], 3))
    row, lane = iotas((CL_DEV * RHS, CL_DEV))
    eight = ones_where(row // RHS == lane)
    wide = sum(dot(eight, part, (1, 0)) for part in split(rowcoef, 3))
    row, lane = iotas(wide.shape)
    wide = jnp.where(lax.rem(row, RHS) == lax.rem(lane, RHS), wide, 0.0)
    row, lane = iotas((128, RANK))
    narrow = ones_where(row // RHS == lane)
    rows = sum(dot(part, narrow, (1, 0)) for part in split(wide, 3))
    rows_high = rows.astype(BF16).astype(F32)
    lefts = jnp.concatenate([rows_high, rows_high, rows - rows_high], axis=1)
    for load in loads[1:]:
        load.wait()
    for c in range(CL_DEV):
        block = basis[:, cluster_cols(c)]
        high = block.astype(BF16).astype(F32)
        parts = jnp.concatenate([high, block - high, high], axis=0).astype(BF16)
        near[c] = self_sum[c] + dot(lefts[c * RHS : (c + 1) * RHS].astype(BF16), parts, (1, 0))

    def add_local(t, carry):
        slot = jnp.where(t < EARLY, t, t + CROSS_DEV)
        near[local_pairs[0, t]] += first_sum[slot]
        near[local_pairs[1, t]] += second_sum[slot]
        return carry

    lax.fori_loop(0, LOC_DEV, add_local, 0)

    def add_cross(t, carry):
        near[cross_pairs[0, t]] += first_sum[EARLY + t]
        return carry

    lax.fori_loop(0, cross_count[0], add_cross, 0)

    def add_returned(t, carry):
        near[info_in[1, t]] += returned[t]
        return carry

    lax.fori_loop(0, info_in[2, 0], add_returned, 0)
    for c in range(CL_DEV):
        cols = cluster_cols(c)
        out[:, cols] = near[c] * (weight[:, cols] * FOUR_PI_INV)


def on_device(
    positions, panel_weight, charges, basis, proxies, local_pairs, cross_pairs, cross_count, far_blocks
):
    panels = positions.shape[1]
    weight = panel_weight.reshape(1, panels)
    vmem = pl.BlockSpec(memory_space=pltpu.VMEM)
    smem = pl.BlockSpec(memory_space=pltpu.SMEM)
    hbm = pl.BlockSpec(memory_space=pltpu.HBM)

    def floats(*shape):
        return pltpu.VMEM(shape, F32)

    outs = pl.pallas_call(
        near_kernel,
        out_shape=[
            jax.ShapeDtypeStruct((CL_DEV, RHS, CLUSTER), F32),
            jax.ShapeDtypeStruct((PAIRS, RHS, CLUSTER), F32),
            jax.ShapeDtypeStruct((PAIRS, RHS, CLUSTER), F32),
            jax.ShapeDtypeStruct((N_ZC, N_X, N_Y, ROWS, 128), F32),
            jax.ShapeDtypeStruct((CROSS_DEV, RHS, CLUSTER), F32),
            jax.ShapeDtypeStruct((8, 128), jnp.int32),
            jax.ShapeDtypeStruct((CL_DEV, 128), F32),
        ],
        in_specs=[hbm] * 4 + [vmem] * 3 + [smem] * 3,
        out_specs=[hbm] * 6 + [vmem],
        scratch_shapes=[
            floats(CL_DEV, RHS, CLUSTER),
            floats(PAIRS, RHS, CLUSTER),
            floats(PAIRS, RHS, CLUSTER),
            floats(3, panels),
            floats(1, panels),
            floats(RHS, panels),
            floats(RANK, panels),
            pltpu.VMEM((CL_DEV + EDGE, 2 * RHS, CLUSTER), BF16),
            floats(CL_DEV + EDGE, 8, CLUSTER),
            floats(CL_DEV, CLUSTER, 8),
            floats(CL_DEV * 2 * RANK, 2 * RHS),
            floats(FAR_DEV, 128),
            floats(FAR_DEV, 128),
            floats(DEVICES * ROWS, 128),
            floats(N_Y, N_X * N_ZC * ROWS, 128),
            floats(N_X, N_Y, N_ZC * ROWS, 128),
            floats(RHS, EDGE_PANELS),
            floats(3, EDGE_PANELS),
            floats(RHS, EDGE_PANELS),
            pltpu.VMEM((8, 128), jnp.int32),
        ]
        + [pltpu.VMEM((CLUSTER, CLUSTER), BF16)] * 4
        + [pltpu.SemaphoreType.DMA((count,)) for count in (4, 13, 13, 3, 4, 4, 7)],
        compiler_params=pltpu.CompilerParams(
            collective_id=0, has_side_effects=True, vmem_limit_bytes=60 * 2**20
        ),
    )(
        positions, weight, charges, basis, proxies, far_blocks, cross_pairs, local_pairs, cross_pairs, cross_count
    )
    self_sum, first_sum, second_sum, far_in, returned, info_in, proxy_table = outs
    return pl.pallas_call(
        far_kernel,
        out_shape=jax.ShapeDtypeStruct((RHS, panels), F32),
        in_specs=[hbm, vmem] + [hbm] * 6 + [smem] * 4,
        out_specs=vmem,
        scratch_shapes=[
            floats(CL_DEV, RHS, CLUSTER),
            floats(DEVICES * ROWS, 128),
            floats(RANK, panels),
            floats(1, panels),
            floats(CL_DEV, RHS, CLUSTER),
            floats(PAIRS, RHS, CLUSTER),
            floats(PAIRS, RHS, CLUSTER),
            floats(CROSS_DEV, RHS, CLUSTER),
            floats(128, FAR_DEV),
            floats(128, FAR_DEV),
            floats(RANK * RANK, FAR_DEV),
            floats(128, FAR_DEV),
            pltpu.SemaphoreType.DMA((7,)),
        ],
        compiler_params=pltpu.CompilerParams(vmem_limit_bytes=60 * 2**20),
    )(
        far_in.reshape(-1, 128), proxy_table, basis, weight, self_sum, first_sum, second_sum,
        returned, local_pairs, cross_pairs, cross_count, info_in,
    )


def solution(mesh):
    whole = P(None, ("gx", "gy"))
    flat = P(("gx", "gy"))
    return jax.shard_map(
        on_device,
        mesh=mesh,
        in_specs=(whole, flat, whole, whole, whole, whole, whole, flat, whole),
        out_specs=whole,
        check_vma=False,
    )
```

```python
import functools

import jax
import jax.numpy as jnp
from jax import lax
from jax.experimental import pallas as pl
from jax.experimental.pallas import tpu as pltpu
from jax.sharding import PartitionSpec as P

CLUSTER = 512
RANK = 16
RHS = 8
EDGE = 8
FOUR_PI_INV = 0.07957747154594767
SOFTENING = 0.0025
CL_DEV = 32
LOC_DEV = 32
CROSS_DEV = 16
PAIRS = CROSS_DEV + LOC_DEV
EARLY = 8
FAR_DEV = 256
EDGE_PANELS = EDGE * CLUSTER
SELF_CHUNK = 32
PAIR_CHUNK = 16
STRIP = 128
DEVICES = 128
N_Y, N_X, N_ZC = 4, 4, 8
ROWS = 8
MESH = pl.DeviceIdType.MESH
F32 = jnp.float32
BF16 = jnp.bfloat16


def dot(a, b, dims):
    return lax.dot_general(a, b, ((dims[:1], dims[1:]), ((), ())), preferred_element_type=F32)


def split(value, parts):
    out = []
    for _ in range(parts - 1):
        high = value.astype(BF16)
        out.append(high)
        value = value - high.astype(F32)
    out.append(value.astype(BF16))
    return out


def split_rows(value):
    high = value.astype(BF16).astype(F32)
    return jnp.concatenate([high, value - high], axis=0).astype(BF16)


def iotas(shape):
    return lax.broadcasted_iota(jnp.int32, shape, 0), lax.broadcasted_iota(jnp.int32, shape, 1)


def ones_where(condition):
    return jnp.where(condition, 1.0, 0.0).astype(BF16)


def cluster_cols(c):
    return slice(c * CLUSTER, (c + 1) * CLUSTER)


def near_kernel(
    pos_hbm, weight_hbm, charges_hbm, basis_hbm, proxies, far_blocks, cross_vector, local_pairs, cross_pairs, cross_count,
    self_out, first_out, second_out, far_in, returned, info_in, proxy_table,
    self_sum, first_sum, second_sum, pos, weight, charges, basis, cw, pos_c, pos_t, moments, coef_rows, proxy_rows, send, recv, head_w, next_pos, next_w,
    info, hi0, hi1, lo0, lo1, load_sem, far_send, far_recv, far_own, edge_send, edge_recv, out_sem,
):
    y = lax.axis_index("gx")
    gy = lax.axis_index("gy")
    x = gy // N_ZC
    zc = lax.rem(gy, N_ZC)
    flat = y * (N_X * N_ZC) + gy
    tile_hi, tile_lo = (hi0, hi1), (lo0, lo1)

    loads = [
        pltpu.make_async_copy(source, target, load_sem.at[i])
        for i, (source, target) in enumerate(
            ((weight_hbm, weight), (charges_hbm, charges), (pos_hbm, pos), (basis_hbm, basis))
        )
    ]
    for load in loads:
        load.start()

    def device_of(index):
        return (index // (N_X * N_ZC), lax.rem(index, N_X * N_ZC))

    after = device_of(lax.rem(flat + 1, DEVICES))
    before = device_of(lax.rem(flat + DEVICES - 1, DEVICES))
    chips = [(lax.rem(y + i // N_X, N_Y), lax.rem(x + i % N_X, N_X)) for i in range(1, N_Y * N_X)]
    peers = [(to_y, to_x * N_ZC + zc) for to_y, to_x in chips] + [
        (y, x * N_ZC + lax.rem(zc + i, N_ZC)) for i in range(1, N_ZC)
    ]
    barrier = pltpu.get_barrier_semaphore()
    for peer in peers + [after, before]:
        pl.semaphore_signal(barrier, inc=1, device_id=peer, device_id_type=MESH)

    info[...] = jnp.zeros_like(info)
    info[0:2, 0:CROSS_DEV] = cross_vector[...]
    info[2:3, :] = jnp.full((1, 128), cross_count[0], jnp.int32)

    columns = jnp.concatenate([proxies[...], jnp.zeros((5, CL_DEV * RANK), F32)], axis=0).T
    row, lane = iotas((CL_DEV * RANK, 128))
    spread = jnp.where(
        lane < RANK, columns[:, 0:1], jnp.where(lane < 2 * RANK, columns[:, 1:2], columns[:, 2:3])
    )
    spread = jnp.where((lax.rem(row, RANK) == lax.rem(lane, RANK)) & (lane < 3 * RANK), spread, 0.0)
    row, lane = iotas((CL_DEV, CL_DEV * RANK))
    gather = ones_where(row == lane // RANK)
    table = sum(dot(gather, part, (1, 0)) for part in split(spread, 3))
    proxy_table[...] = table

    for load in loads:
        load.wait()
    for c in range(CL_DEV):
        cols = cluster_cols(c)
        parts = split_rows(charges[:, cols] * weight[:, cols])
        cw[c] = parts
        place = jnp.concatenate([pos[:, cols], jnp.zeros((5, CLUSTER), F32)], axis=0)
        pos_c[c] = place
        pos_t[c] = place.T
        moments[c * 32 : (c + 1) * 32, :] = dot(split_rows(basis[:, cols]), parts, (1, 1))
    head_w[...] = charges[:, :EDGE_PANELS] * weight[:, :EDGE_PANELS]

    row, lane = iotas((2 * RHS, 128))
    spread = ones_where(lax.rem(row, RHS) == lax.rem(lane, RHS))
    wide = sum(dot(part, spread, (1, 0)) for part in split(moments[...], 3))
    row, lane = iotas(wide.shape)
    wide = jnp.where(lax.rem(row, RANK) == lane // RHS, wide, 0.0)
    coef = jnp.sum(wide.reshape(CL_DEV, 2 * RANK, 128), axis=1)

    row, lane = iotas((CL_DEV, 256))
    numbers = jnp.where(lane == 128 + 3 * RANK, row.astype(F32), 0.0).astype(BF16)
    both = jnp.concatenate(split(jnp.concatenate([coef, table], axis=1), 3) + [numbers], axis=0)
    row, lane = iotas((3 * CL_DEV, FAR_DEV))
    pick_source = jnp.where(lax.rem(row, CL_DEV) == far_blocks[0:1, :], 1.0, 0.0)
    row, lane = iotas((CL_DEV, FAR_DEV))
    pick_number = jnp.where(row == (far_blocks[1:2, :] & (CL_DEV - 1)), 1.0, 0.0)
    pick = jnp.concatenate([pick_source, pick_number], axis=0).astype(BF16)
    picked = dot(pick, both, (0, 0))
    coef_rows[...] = picked[:, :128]
    proxy_rows[...] = picked[:, 128:]
    for j in range(2):
        send[pl.ds(j, DEVICES, stride=ROWS), :] = coef_rows[pl.ds(j, DEVICES, stride=2), :]
        for k in range(2, ROWS, 2):
            send[pl.ds(k + j, DEVICES, stride=ROWS), :] = proxy_rows[pl.ds(j, DEVICES, stride=2), :]

    def far_copy(source, target, index, peer):
        return pltpu.make_async_remote_copy(
            src_ref=source, dst_ref=target, send_sem=far_send.at[index], recv_sem=far_recv.at[index],
            device_id=peer, device_id_type=MESH,
        )

    def edge_copy(source, target, index, peer):
        return pltpu.make_async_remote_copy(
            src_ref=source, dst_ref=target, send_sem=edge_send.at[index], recv_sem=edge_recv.at[index],
            device_id=peer, device_id_type=MESH,
        )

    def start(copies):
        for copy in copies:
            copy.start()

    def wait(copies):
        for copy in copies:
            copy.wait()

    def part(index, count):
        return pl.ds(pl.multiple_of(index * count, count), count)

    per_chip = N_ZC * ROWS
    phase1 = [pltpu.make_async_copy(send.at[part(y * N_X + x, per_chip)], recv.at[0], far_own.at[0])] + [
        far_copy(send.at[part(to_y * N_X + to_x, per_chip)], recv.at[i + 1], i, peers[i])
        for i, (to_y, to_x) in enumerate(chips)
    ]
    phase2 = [pltpu.make_async_copy(recv.at[:, part(zc, ROWS)], far_in.at[0], far_own.at[1])] + [
        far_copy(recv.at[:, part(lax.rem(zc + i, N_ZC), ROWS)], far_in.at[i], len(chips) + i - 1, peers[len(chips) + i - 1])
        for i in range(1, N_ZC)
    ]
    heads = [
        edge_copy(pos.at[:, pl.ds(0, EDGE_PANELS)], next_pos, 0, before),
        edge_copy(head_w, next_w, 1, before),
        edge_copy(info, info_in, 2, after),
    ]
    crossing = pl.ds(EARLY, CROSS_DEV)
    give_back = edge_copy(second_sum.at[crossing], returned, 3, after)
    gives, gets = flat < DEVICES - 1, flat > 0

    def out_copies(index, first, count, *pairs):
        rows = pl.ds(first, count)
        return [
            pltpu.make_async_copy(source.at[rows], target.at[rows], out_sem.at[index + i])
            for i, (source, target) in enumerate(pairs)
        ]

    first_pair, second_pair = (first_sum, first_out), (second_sum, second_out)
    done = EARLY + CROSS_DEV
    outs_self = out_copies(0, 0, CL_DEV, (self_sum, self_out))
    outs_early = out_copies(1, 0, done, first_pair) + out_copies(2, 0, EARLY, second_pair)
    outs_late = out_copies(3, done, 16, first_pair, second_pair)
    outs_last = out_copies(5, done + 16, 8, first_pair, second_pair)

    def fill(row_cluster, columns, slot, row_from, row_to, col_from, chunk):
        col_x = pos_c[columns, 0:1, col_from:]
        col_y = pos_c[columns, 1:2, col_from:]
        col_z = pos_c[columns, 2:3, col_from:]
        for begin in range(row_from, row_to, chunk):
            rows = pos_t[row_cluster, begin : begin + chunk, :]
            dx = rows[:, 0:1] - col_x
            dy = rows[:, 1:2] - col_y
            dz = rows[:, 2:3] - col_z
            value = lax.rsqrt(dx * dx + dy * dy + dz * dz + SOFTENING)
            high = value.astype(BF16)
            tile_hi[slot][begin : begin + chunk, col_from:] = high
            tile_lo[slot][begin : begin + chunk, col_from:] = (value - high.astype(F32)).astype(BF16)

    def halves(parts, slot, rows, cols, side):
        sums = dot(parts, tile_hi[slot][rows, cols], (1, side)) + dot(parts, tile_lo[slot][rows, cols], (1, side))
        return sums[:RHS] + sums[RHS:]

    whole = slice(0, CLUSTER)

    def self_compute(t, slot):
        for begin in range(0, CLUSTER, STRIP):
            fill(t, t, slot, begin, begin + STRIP, begin, SELF_CHUNK)

    def self_apply(t, slot):
        parts = cw[t]
        sums = [None] * (CLUSTER // STRIP)
        for i in range(CLUSTER // STRIP):
            rows = slice(i * STRIP, (i + 1) * STRIP)
            down = halves(parts[:, rows], slot, rows, slice(i * STRIP, CLUSTER), 0)
            for j in range(i, CLUSTER // STRIP):
                piece = down[:, (j - i) * STRIP : (j - i + 1) * STRIP]
                sums[j] = piece if sums[j] is None else sums[j] + piece
            if i + 1 < CLUSTER // STRIP:
                rest = slice((i + 1) * STRIP, CLUSTER)
                sums[i] = sums[i] + halves(parts[:, rest], slot, rows, rest, 1)
        self_sum[t] = jnp.concatenate(sums, axis=1)

    def pair_of(t):
        crosses = (t >= EARLY) & (t < done)
        c = jnp.clip(t - EARLY, 0, CROSS_DEV - 1)
        l = jnp.clip(jnp.where(t < EARLY, t, t - CROSS_DEV), 0, LOC_DEV - 1)
        first = jnp.where(crosses, cross_pairs[0, c], local_pairs[0, l])
        second = jnp.where(crosses, cross_pairs[1, c] + CL_DEV, local_pairs[1, l])
        return first, second

    def pair_compute(t, slot):
        first, second = pair_of(t)
        fill(first, second, slot, 0, CLUSTER, 0, PAIR_CHUNK)

    def pair_apply(t, slot):
        first, second = pair_of(t)
        first_sum[t] = halves(cw[second], slot, whole, whole, 1)
        second_sum[t] = halves(cw[first], slot, whole, whole, 0)

    def section(count, compute, apply, steps):
        compute(0, 0)

        def body(i, carry):
            for at, step in steps:
                pl.when(i == at)(step)
            compute(2 * i + 1, 1)
            apply(2 * i, 0)
            compute(jnp.minimum(2 * i + 2, count - 1), 0)
            apply(2 * i + 1, 1)
            return carry

        lax.fori_loop(0, count // 2, body, 0)

    def send_first():
        pl.semaphore_wait(barrier, len(peers) + 2)
        start(heads)

    def take_heads():
        wait(heads)
        for j in range(EDGE):
            cw[CL_DEV + j] = split_rows(next_w[:, cluster_cols(j)])
            pos_c[CL_DEV + j, 0:3, :] = next_pos[:, cluster_cols(j)]

    def send_last():
        wait(phase1)
        start(phase2)

    def send_back():
        pl.when(gives)(give_back.start)
        start(outs_early)

    section(CL_DEV, self_compute, self_apply, [(6, send_first), (8, lambda: start(phase1))])
    start(outs_self)
    section(
        PAIRS,
        pair_compute,
        pair_apply,
        [(EARLY // 2 - 1, take_heads), (8, send_last), (done // 2, send_back), (done // 2 + 8, lambda: start(outs_late))],
    )
    start(outs_last)
    wait(outs_self)
    wait(outs_early)
    wait(outs_late)
    wait(phase2)
    pl.when(gives)(give_back.wait_send)
    pl.when(gets)(give_back.wait_recv)
    wait(outs_last)


def far_kernel(
    far_hbm, proxy_table, basis_hbm, weight_hbm, self_hbm, first_hbm, second_hbm, returned_hbm,
    local_pairs, cross_pairs, cross_count, info_in,
    out, near, far_in, basis, weight, self_sum, first_sum, second_sum, returned, coef, target, coupling, contrib, load_sem,
):
    loads = [
        pltpu.make_async_copy(source, target, load_sem.at[i])
        for i, (source, target) in enumerate(
            (
                (far_hbm, far_in),
                (basis_hbm, basis),
                (self_hbm, self_sum),
                (first_hbm, first_sum),
                (second_hbm, second_sum),
                (returned_hbm, returned),
                (weight_hbm, weight),
            )
        )
    ]
    for load in loads:
        load.start()
    loads[0].wait()

    def strided(j):
        return far_in[pl.ds(j, DEVICES, stride=ROWS), :]

    coef[...] = jnp.concatenate([strided(0).T, strided(1).T], axis=1)
    source = jnp.concatenate([strided(2).T, strided(3).T], axis=1)
    number = source[3 * RANK : 3 * RANK + 1, :].astype(jnp.int32)
    row, lane = iotas((CL_DEV, FAR_DEV))
    pick = ones_where(row == number)
    target[...] = sum(dot(part, pick, (0, 0)) for part in split(proxy_table[...], 3))
    for k in range(RANK):
        distance = SOFTENING
        for axis in range(3):
            end = axis * RANK + k
            offset = target[end : end + 1, :] - source[axis * RANK : (axis + 1) * RANK, :]
            distance = distance + offset * offset
        coupling[k * RANK : (k + 1) * RANK, :] = lax.rsqrt(distance)
    for k in range(RANK):
        total = None
        for l in range(RANK):
            entry = k * RANK + l
            term = coupling[entry : entry + 1, :] * coef[l * RHS : (l + 1) * RHS, :]
            total = term if total is None else total + term
        contrib[k * RHS : (k + 1) * RHS, :] = total
    rowcoef = sum(dot(pick, part, (1, 1)) for part in split(contrib[...], 3))
    row, lane = iotas((CL_DEV * RHS, CL_DEV))
    eight = ones_where(row // RHS == lane)
    wide = sum(dot(eight, part, (1, 0)) for part in split(rowcoef, 3))
    row, lane = iotas(wide.shape)
    wide = jnp.where(lax.rem(row, RHS) == lax.rem(lane, RHS), wide, 0.0)
    row, lane = iotas((128, RANK))
    narrow = ones_where(row // RHS == lane)
    rows = sum(dot(part, narrow, (1, 0)) for part in split(wide, 3))
    rows_high = rows.astype(BF16).astype(F32)
    lefts = jnp.concatenate([rows_high, rows_high, rows - rows_high], axis=1)
    for load in loads[1:]:
        load.wait()
    for c in range(CL_DEV):
        block = basis[:, cluster_cols(c)]
        high = block.astype(BF16).astype(F32)
        parts = jnp.concatenate([high, block - high, high], axis=0).astype(BF16)
        near[c] = self_sum[c] + dot(lefts[c * RHS : (c + 1) * RHS].astype(BF16), parts, (1, 0))

    def add_local(t, carry):
        slot = jnp.where(t < EARLY, t, t + CROSS_DEV)
        near[local_pairs[0, t]] += first_sum[slot]
        near[local_pairs[1, t]] += second_sum[slot]
        return carry

    lax.fori_loop(0, LOC_DEV, add_local, 0, unroll=8)

    def add_cross(t, carry):
        near[cross_pairs[0, t]] += first_sum[EARLY + t]
        return carry

    lax.fori_loop(0, cross_count[0], add_cross, 0)

    def add_returned(t, carry):
        near[info_in[1, t]] += returned[t]
        return carry

    lax.fori_loop(0, info_in[2, 0], add_returned, 0)
    for c in range(CL_DEV):
        cols = cluster_cols(c)
        out[:, cols] = near[c] * (weight[:, cols] * FOUR_PI_INV)


def on_device(
    positions, panel_weight, charges, basis, proxies, local_pairs, cross_pairs, cross_count, far_blocks
):
    panels = positions.shape[1]
    weight = panel_weight.reshape(1, panels)
    vmem = pl.BlockSpec(memory_space=pltpu.VMEM)
    smem = pl.BlockSpec(memory_space=pltpu.SMEM)
    hbm = pl.BlockSpec(memory_space=pltpu.HBM)

    def floats(*shape):
        return pltpu.VMEM(shape, F32)

    outs = pl.pallas_call(
        near_kernel,
        out_shape=[
            jax.ShapeDtypeStruct((CL_DEV, RHS, CLUSTER), F32),
            jax.ShapeDtypeStruct((PAIRS, RHS, CLUSTER), F32),
            jax.ShapeDtypeStruct((PAIRS, RHS, CLUSTER), F32),
            jax.ShapeDtypeStruct((N_ZC, N_Y * N_X, ROWS, 128), F32),
            jax.ShapeDtypeStruct((CROSS_DEV, RHS, CLUSTER), F32),
            jax.ShapeDtypeStruct((8, 128), jnp.int32),
            jax.ShapeDtypeStruct((CL_DEV, 128), F32),
        ],
        in_specs=[hbm] * 4 + [vmem] * 3 + [smem] * 3,
        out_specs=[hbm] * 6 + [vmem],
        scratch_shapes=[
            floats(CL_DEV, RHS, CLUSTER),
            floats(PAIRS, RHS, CLUSTER),
            floats(PAIRS, RHS, CLUSTER),
            floats(3, panels),
            floats(1, panels),
            floats(RHS, panels),
            floats(RANK, panels),
            pltpu.VMEM((CL_DEV + EDGE, 2 * RHS, CLUSTER), BF16),
            floats(CL_DEV + EDGE, 8, CLUSTER),
            floats(CL_DEV, CLUSTER, 8),
            floats(CL_DEV * 2 * RANK, 2 * RHS),
            floats(FAR_DEV, 128),
            floats(FAR_DEV, 128),
            floats(DEVICES * ROWS, 128),
            floats(N_Y * N_X, N_ZC * ROWS, 128),
            floats(RHS, EDGE_PANELS),
            floats(3, EDGE_PANELS),
            floats(RHS, EDGE_PANELS),
            pltpu.VMEM((8, 128), jnp.int32),
        ]
        + [pltpu.VMEM((CLUSTER, CLUSTER), BF16)] * 4
        + [pltpu.SemaphoreType.DMA((count,)) for count in (4, 22, 22, 2, 4, 4, 7)],
        compiler_params=pltpu.CompilerParams(
            collective_id=0, has_side_effects=True, vmem_limit_bytes=60 * 2**20
        ),
    )(
        positions, weight, charges, basis, proxies, far_blocks, cross_pairs, local_pairs, cross_pairs, cross_count
    )
    self_sum, first_sum, second_sum, far_in, returned, info_in, proxy_table = outs
    return pl.pallas_call(
        far_kernel,
        out_shape=jax.ShapeDtypeStruct((RHS, panels), F32),
        in_specs=[hbm, vmem] + [hbm] * 6 + [smem] * 4,
        out_specs=vmem,
        scratch_shapes=[
            floats(CL_DEV, RHS, CLUSTER),
            floats(DEVICES * ROWS, 128),
            floats(RANK, panels),
            floats(1, panels),
            floats(CL_DEV, RHS, CLUSTER),
            floats(PAIRS, RHS, CLUSTER),
            floats(PAIRS, RHS, CLUSTER),
            floats(CROSS_DEV, RHS, CLUSTER),
            floats(128, FAR_DEV),
            floats(128, FAR_DEV),
            floats(RANK * RANK, FAR_DEV),
            floats(128, FAR_DEV),
            pltpu.SemaphoreType.DMA((7,)),
        ],
        compiler_params=pltpu.CompilerParams(vmem_limit_bytes=60 * 2**20),
    )(
        far_in.reshape(-1, 128), proxy_table, basis, weight, self_sum, first_sum, second_sum,
        returned, local_pairs, cross_pairs, cross_count, info_in,
    )


def solution(mesh):
    whole = P(None, ("gx", "gy"))
    flat = P(("gx", "gy"))
    return jax.shard_map(
        on_device,
        mesh=mesh,
        in_specs=(whole, flat, whole, whole, whole, whole, whole, flat, whole),
        out_specs=whole,
        check_vma=False,
    )
```

```python
import functools

import jax
import jax.numpy as jnp
from jax import lax
from jax.experimental import pallas as pl
from jax.experimental.pallas import tpu as pltpu
from jax.sharding import PartitionSpec as P

CLUSTER = 512
RANK = 16
RHS = 8
EDGE = 8
FOUR_PI_INV = 0.07957747154594767
SOFTENING = 0.0025
CL_DEV = 32
LOC_DEV = 32
CROSS_DEV = 16
PAIRS = CROSS_DEV + LOC_DEV
EARLY = 8
FAR_DEV = 256
EDGE_PANELS = EDGE * CLUSTER
SELF_CHUNK = 32
PAIR_CHUNK = 16
STRIP = 128
DEVICES = 128
N_Y, N_X, N_ZC = 4, 4, 8
ROWS = 8
MESH = pl.DeviceIdType.MESH
F32 = jnp.float32
BF16 = jnp.bfloat16


def dot(a, b, dims):
    return lax.dot_general(a, b, ((dims[:1], dims[1:]), ((), ())), preferred_element_type=F32)


def split(value, parts):
    out = []
    for _ in range(parts - 1):
        high = value.astype(BF16)
        out.append(high)
        value = value - high.astype(F32)
    out.append(value.astype(BF16))
    return out


def split_rows(value):
    high = value.astype(BF16).astype(F32)
    return jnp.concatenate([high, value - high], axis=0).astype(BF16)


def iotas(shape):
    return lax.broadcasted_iota(jnp.int32, shape, 0), lax.broadcasted_iota(jnp.int32, shape, 1)


def ones_where(condition):
    return jnp.where(condition, 1.0, 0.0).astype(BF16)


def cluster_cols(c):
    return slice(c * CLUSTER, (c + 1) * CLUSTER)


def near_kernel(
    pos_hbm, weight_hbm, charges_hbm, basis_hbm, proxies, far_blocks, cross_vector, local_pairs, cross_pairs, cross_count,
    self_out, first_out, second_out, far_in, returned, info_in, proxy_table,
    self_sum, first_sum, second_sum, pos, weight, charges, basis, cw, pos_c, pos_t, moments, coef_rows, proxy_rows, send, recv, head_w, next_pos, next_w,
    info, hi0, hi1, lo0, lo1, load_sem, far_send, far_recv, far_own, edge_send, edge_recv, out_sem,
):
    y = lax.axis_index("gx")
    gy = lax.axis_index("gy")
    x = gy // N_ZC
    zc = lax.rem(gy, N_ZC)
    flat = y * (N_X * N_ZC) + gy
    tile_hi, tile_lo = (hi0, hi1), (lo0, lo1)

    loads = [
        pltpu.make_async_copy(source, target, load_sem.at[i])
        for i, (source, target) in enumerate(
            ((weight_hbm, weight), (charges_hbm, charges), (pos_hbm, pos), (basis_hbm, basis))
        )
    ]
    for load in loads:
        load.start()

    def device_of(index):
        return (index // (N_X * N_ZC), lax.rem(index, N_X * N_ZC))

    after = device_of(lax.rem(flat + 1, DEVICES))
    before = device_of(lax.rem(flat + DEVICES - 1, DEVICES))
    chips = [(lax.rem(y + i // N_X, N_Y), lax.rem(x + i % N_X, N_X)) for i in range(1, N_Y * N_X)]
    peers = [(to_y, to_x * N_ZC + zc) for to_y, to_x in chips] + [
        (y, x * N_ZC + lax.rem(zc + i, N_ZC)) for i in range(1, N_ZC)
    ]
    barrier = pltpu.get_barrier_semaphore()
    for peer in peers + [after, before]:
        pl.semaphore_signal(barrier, inc=1, device_id=peer, device_id_type=MESH)

    info[...] = jnp.zeros_like(info)
    info[0:2, 0:CROSS_DEV] = cross_vector[...]
    info[2:3, :] = jnp.full((1, 128), cross_count[0], jnp.int32)

    columns = jnp.concatenate([proxies[...], jnp.zeros((5, CL_DEV * RANK), F32)], axis=0).T
    row, lane = iotas((CL_DEV * RANK, 128))
    spread = jnp.where(
        lane < RANK, columns[:, 0:1], jnp.where(lane < 2 * RANK, columns[:, 1:2], columns[:, 2:3])
    )
    spread = jnp.where((lax.rem(row, RANK) == lax.rem(lane, RANK)) & (lane < 3 * RANK), spread, 0.0)
    row, lane = iotas((CL_DEV, CL_DEV * RANK))
    gather = ones_where(row == lane // RANK)
    table = sum(dot(gather, part, (1, 0)) for part in split(spread, 3))
    proxy_table[...] = table

    for load in loads:
        load.wait()
    for c in range(CL_DEV):
        cols = cluster_cols(c)
        parts = split_rows(charges[:, cols] * weight[:, cols])
        cw[c] = parts
        place = jnp.concatenate([pos[:, cols], jnp.zeros((5, CLUSTER), F32)], axis=0)
        pos_c[c] = place
        pos_t[c] = place.T
        moments[c * 32 : (c + 1) * 32, :] = dot(split_rows(basis[:, cols]), parts, (1, 1))
    head_w[...] = charges[:, :EDGE_PANELS] * weight[:, :EDGE_PANELS]

    row, lane = iotas((2 * RHS, 128))
    spread = ones_where(lax.rem(row, RHS) == lax.rem(lane, RHS))
    wide = sum(dot(part, spread, (1, 0)) for part in split(moments[...], 3))
    row, lane = iotas(wide.shape)
    wide = jnp.where(lax.rem(row, RANK) == lane // RHS, wide, 0.0)
    coef = jnp.sum(wide.reshape(CL_DEV, 2 * RANK, 128), axis=1)

    row, lane = iotas((CL_DEV, 256))
    numbers = jnp.where(lane == 128 + 3 * RANK, row.astype(F32), 0.0).astype(BF16)
    both = jnp.concatenate(split(jnp.concatenate([coef, table], axis=1), 3) + [numbers], axis=0)
    row, lane = iotas((3 * CL_DEV, FAR_DEV))
    pick_source = jnp.where(lax.rem(row, CL_DEV) == far_blocks[0:1, :], 1.0, 0.0)
    row, lane = iotas((CL_DEV, FAR_DEV))
    pick_number = jnp.where(row == (far_blocks[1:2, :] & (CL_DEV - 1)), 1.0, 0.0)
    pick = jnp.concatenate([pick_source, pick_number], axis=0).astype(BF16)
    picked = dot(pick, both, (0, 0))
    coef_rows[...] = picked[:, :128]
    proxy_rows[...] = picked[:, 128:]
    for j in range(2):
        send[pl.ds(j, DEVICES, stride=ROWS), :] = coef_rows[pl.ds(j, DEVICES, stride=2), :]
        for k in range(2, ROWS, 2):
            send[pl.ds(k + j, DEVICES, stride=ROWS), :] = proxy_rows[pl.ds(j, DEVICES, stride=2), :]

    def far_copy(source, target, index, peer):
        return pltpu.make_async_remote_copy(
            src_ref=source, dst_ref=target, send_sem=far_send.at[index], recv_sem=far_recv.at[index],
            device_id=peer, device_id_type=MESH,
        )

    def edge_copy(source, target, index, peer):
        return pltpu.make_async_remote_copy(
            src_ref=source, dst_ref=target, send_sem=edge_send.at[index], recv_sem=edge_recv.at[index],
            device_id=peer, device_id_type=MESH,
        )

    def start(copies):
        for copy in copies:
            copy.start()

    def wait(copies):
        for copy in copies:
            copy.wait()

    def part(index, count):
        return pl.ds(pl.multiple_of(index * count, count), count)

    per_chip = N_ZC * ROWS
    phase1 = [pltpu.make_async_copy(send.at[part(y * N_X + x, per_chip)], recv.at[0], far_own.at[0])] + [
        far_copy(send.at[part(to_y * N_X + to_x, per_chip)], recv.at[i + 1], i, peers[i])
        for i, (to_y, to_x) in enumerate(chips)
    ]
    phase2 = [pltpu.make_async_copy(recv.at[:, part(zc, ROWS)], far_in.at[0], far_own.at[1])] + [
        far_copy(recv.at[:, part(lax.rem(zc + i, N_ZC), ROWS)], far_in.at[i], len(chips) + i - 1, peers[len(chips) + i - 1])
        for i in range(1, N_ZC)
    ]
    heads = [
        edge_copy(pos.at[:, pl.ds(0, EDGE_PANELS)], next_pos, 0, before),
        edge_copy(head_w, next_w, 1, before),
        edge_copy(info, info_in, 2, after),
    ]
    crossing = pl.ds(EARLY, CROSS_DEV)
    give_back = edge_copy(second_sum.at[crossing], returned, 3, after)
    gives, gets = flat < DEVICES - 1, flat > 0

    def out_copies(index, first, count, *pairs):
        rows = pl.ds(first, count)
        return [
            pltpu.make_async_copy(source.at[rows], target.at[rows], out_sem.at[index + i])
            for i, (source, target) in enumerate(pairs)
        ]

    first_pair, second_pair = (first_sum, first_out), (second_sum, second_out)
    done = EARLY + CROSS_DEV
    outs_self = out_copies(0, 0, CL_DEV, (self_sum, self_out))
    outs_early = out_copies(1, 0, done, first_pair) + out_copies(2, 0, EARLY, second_pair)
    outs_late = out_copies(3, done, 16, first_pair, second_pair)
    outs_last = out_copies(5, done + 16, 8, first_pair, second_pair)

    def fill(row_cluster, columns, slot, row_from, row_to, col_from, chunk):
        col_x = pos_c[columns, 0:1, col_from:]
        col_y = pos_c[columns, 1:2, col_from:]
        col_z = pos_c[columns, 2:3, col_from:]
        for begin in range(row_from, row_to, chunk):
            rows = pos_t[row_cluster, begin : begin + chunk, :]
            dx = rows[:, 0:1] - col_x
            dy = rows[:, 1:2] - col_y
            dz = rows[:, 2:3] - col_z
            value = lax.rsqrt(dx * dx + dy * dy + dz * dz + SOFTENING)
            high = value.astype(BF16)
            tile_hi[slot][begin : begin + chunk, col_from:] = high
            tile_lo[slot][begin : begin + chunk, col_from:] = (value - high.astype(F32)).astype(BF16)

    def halves(parts, slot, rows, cols, side):
        sums = dot(parts, tile_hi[slot][rows, cols], (1, side)) + dot(parts, tile_lo[slot][rows, cols], (1, side))
        return sums[:RHS] + sums[RHS:]

    whole = slice(0, CLUSTER)

    def self_compute(t, slot):
        for begin in range(0, CLUSTER, STRIP):
            fill(t, t, slot, begin, begin + STRIP, begin, SELF_CHUNK)

    def self_apply(t, slot):
        parts = cw[t]
        sums = [None] * (CLUSTER // STRIP)
        for i in range(CLUSTER // STRIP):
            rows = slice(i * STRIP, (i + 1) * STRIP)
            down = halves(parts[:, rows], slot, rows, slice(i * STRIP, CLUSTER), 0)
            for j in range(i, CLUSTER // STRIP):
                piece = down[:, (j - i) * STRIP : (j - i + 1) * STRIP]
                sums[j] = piece if sums[j] is None else sums[j] + piece
            if i + 1 < CLUSTER // STRIP:
                rest = slice((i + 1) * STRIP, CLUSTER)
                sums[i] = sums[i] + halves(parts[:, rest], slot, rows, rest, 1)
        self_sum[t] = jnp.concatenate(sums, axis=1)

    def pair_of(t):
        crosses = (t >= EARLY) & (t < done)
        c = jnp.clip(t - EARLY, 0, CROSS_DEV - 1)
        l = jnp.clip(jnp.where(t < EARLY, t, t - CROSS_DEV), 0, LOC_DEV - 1)
        first = jnp.where(crosses, cross_pairs[0, c], local_pairs[0, l])
        second = jnp.where(crosses, cross_pairs[1, c] + CL_DEV, local_pairs[1, l])
        return first, second

    def pair_compute(t, slot):
        first, second = pair_of(t)
        fill(first, second, slot, 0, CLUSTER, 0, PAIR_CHUNK)

    def pair_apply(t, slot):
        first, second = pair_of(t)
        first_sum[t] = halves(cw[second], slot, whole, whole, 1)
        second_sum[t] = halves(cw[first], slot, whole, whole, 0)

    def section(count, compute, apply, steps, after):

        def body(i, carry):
            for at, step in steps:
                pl.when(i == at)(step)
            compute(2 * i + 1, 1)
            apply(2 * i, 0)
            compute(2 * i + 2, 0)
            apply(2 * i + 1, 1)
            return carry

        lax.fori_loop(0, count // 2 - 1, body, 0)
        compute(count - 1, 1)
        apply(count - 2, 0)
        after()
        apply(count - 1, 1)

    def send_first():
        pl.semaphore_wait(barrier, len(peers) + 2)
        start(heads)

    def take_heads():
        wait(heads)
        for j in range(EDGE):
            cw[CL_DEV + j] = split_rows(next_w[:, cluster_cols(j)])
            pos_c[CL_DEV + j, 0:3, :] = next_pos[:, cluster_cols(j)]

    def send_last():
        wait(phase1)
        start(phase2)

    def send_back():
        pl.when(gives)(give_back.start)
        start(outs_early)

    self_compute(0, 0)
    section(CL_DEV, self_compute, self_apply, [(6, send_first), (8, lambda: start(phase1))], lambda: pair_compute(0, 0))
    start(outs_self)
    section(
        PAIRS,
        pair_compute,
        pair_apply,
        [(EARLY // 2 - 1, take_heads), (8, send_last), (done // 2, send_back), (done // 2 + 8, lambda: start(outs_late))],
        lambda: None,
    )
    start(outs_last)
    wait(outs_self)
    wait(outs_early)
    wait(outs_late)
    wait(phase2)
    pl.when(gives)(give_back.wait_send)
    pl.when(gets)(give_back.wait_recv)
    wait(outs_last)


def far_kernel(
    far_hbm, table_hbm, basis_hbm, weight_hbm, self_hbm, first_hbm, second_hbm, returned_hbm,
    local_hbm, cross_hbm, count_hbm, info_hbm,
    out, proxy_table, local_pairs, cross_pairs, cross_count, info_in, near, far_in, basis, weight, self_sum, first_sum, second_sum, returned, coef, target, coupling, contrib, load_sem,
):
    loads = [
        pltpu.make_async_copy(source, target, load_sem.at[i])
        for i, (source, target) in enumerate(
            (
                (far_hbm, far_in),
                (table_hbm, proxy_table),
                (basis_hbm, basis),
                (self_hbm, self_sum),
                (first_hbm, first_sum),
                (second_hbm, second_sum),
                (returned_hbm, returned),
                (weight_hbm, weight),
                (local_hbm, local_pairs),
                (cross_hbm, cross_pairs),
                (count_hbm, cross_count),
                (info_hbm, info_in),
            )
        )
    ]
    for load in loads:
        load.start()
    for load in loads[:2]:
        load.wait()

    def strided(j):
        return far_in[pl.ds(j, DEVICES, stride=ROWS), :]

    coef[...] = jnp.concatenate([strided(0).T, strided(1).T], axis=1)
    source = jnp.concatenate([strided(2).T, strided(3).T], axis=1)
    number = source[3 * RANK : 3 * RANK + 1, :].astype(jnp.int32)
    row, lane = iotas((CL_DEV, FAR_DEV))
    pick = ones_where(row == number)
    target[...] = sum(dot(part, pick, (0, 0)) for part in split(proxy_table[...], 3))
    for k in range(RANK):
        distance = SOFTENING
        for axis in range(3):
            end = axis * RANK + k
            offset = target[end : end + 1, :] - source[axis * RANK : (axis + 1) * RANK, :]
            distance = distance + offset * offset
        coupling[k * RANK : (k + 1) * RANK, :] = lax.rsqrt(distance)
    for k in range(RANK):
        total = None
        for l in range(RANK):
            entry = k * RANK + l
            term = coupling[entry : entry + 1, :] * coef[l * RHS : (l + 1) * RHS, :]
            total = term if total is None else total + term
        contrib[k * RHS : (k + 1) * RHS, :] = total
    rowcoef = sum(dot(pick, part, (1, 1)) for part in split(contrib[...], 3))
    row, lane = iotas((CL_DEV * RHS, CL_DEV))
    eight = ones_where(row // RHS == lane)
    wide = sum(dot(eight, part, (1, 0)) for part in split(rowcoef, 3))
    row, lane = iotas(wide.shape)
    wide = jnp.where(lax.rem(row, RHS) == lax.rem(lane, RHS), wide, 0.0)
    row, lane = iotas((128, RANK))
    narrow = ones_where(row // RHS == lane)
    rows = sum(dot(part, narrow, (1, 0)) for part in split(wide, 3))
    rows_high = rows.astype(BF16).astype(F32)
    lefts = jnp.concatenate([rows_high, rows_high, rows - rows_high], axis=1)
    for load in loads[2:]:
        load.wait()
    for c in range(CL_DEV):
        block = basis[:, cluster_cols(c)]
        high = block.astype(BF16).astype(F32)
        parts = jnp.concatenate([high, block - high, high], axis=0).astype(BF16)
        near[c] = self_sum[c] + dot(lefts[c * RHS : (c + 1) * RHS].astype(BF16), parts, (1, 0))

    def add_local(t, carry):
        slot = jnp.where(t < EARLY, t, t + CROSS_DEV)
        near[local_pairs[0, t]] += first_sum[slot]
        near[local_pairs[1, t]] += second_sum[slot]
        return carry

    lax.fori_loop(0, LOC_DEV, add_local, 0, unroll=8)

    def add_cross(t, carry):
        near[cross_pairs[0, t]] += first_sum[EARLY + t]
        return carry

    lax.fori_loop(0, cross_count[0], add_cross, 0)

    def add_returned(t, carry):
        near[info_in[1, t]] += returned[t]
        return carry

    lax.fori_loop(0, info_in[2, 0], add_returned, 0)
    for c in range(CL_DEV):
        cols = cluster_cols(c)
        out[:, cols] = near[c] * (weight[:, cols] * FOUR_PI_INV)


def on_device(
    positions, panel_weight, charges, basis, proxies, local_pairs, cross_pairs, cross_count, far_blocks
):
    panels = positions.shape[1]
    weight = panel_weight.reshape(1, panels)
    vmem = pl.BlockSpec(memory_space=pltpu.VMEM)
    smem = pl.BlockSpec(memory_space=pltpu.SMEM)
    hbm = pl.BlockSpec(memory_space=pltpu.HBM)

    def floats(*shape):
        return pltpu.VMEM(shape, F32)

    def numbers(*shape):
        return pltpu.SMEM(shape, jnp.int32)

    outs = pl.pallas_call(
        near_kernel,
        out_shape=[
            jax.ShapeDtypeStruct((CL_DEV, RHS, CLUSTER), F32),
            jax.ShapeDtypeStruct((PAIRS, RHS, CLUSTER), F32),
            jax.ShapeDtypeStruct((PAIRS, RHS, CLUSTER), F32),
            jax.ShapeDtypeStruct((N_ZC, N_Y * N_X, ROWS, 128), F32),
            jax.ShapeDtypeStruct((CROSS_DEV, RHS, CLUSTER), F32),
            jax.ShapeDtypeStruct((8, 128), jnp.int32),
            jax.ShapeDtypeStruct((CL_DEV, 128), F32),
        ],
        in_specs=[hbm] * 4 + [vmem] * 3 + [smem] * 3,
        out_specs=[hbm] * 6 + [vmem],
        scratch_shapes=[
            floats(CL_DEV, RHS, CLUSTER),
            floats(PAIRS, RHS, CLUSTER),
            floats(PAIRS, RHS, CLUSTER),
            floats(3, panels),
            floats(1, panels),
            floats(RHS, panels),
            floats(RANK, panels),
            pltpu.VMEM((CL_DEV + EDGE, 2 * RHS, CLUSTER), BF16),
            floats(CL_DEV + EDGE, 8, CLUSTER),
            floats(CL_DEV, CLUSTER, 8),
            floats(CL_DEV * 2 * RANK, 2 * RHS),
            floats(FAR_DEV, 128),
            floats(FAR_DEV, 128),
            floats(DEVICES * ROWS, 128),
            floats(N_Y * N_X, N_ZC * ROWS, 128),
            floats(RHS, EDGE_PANELS),
            floats(3, EDGE_PANELS),
            floats(RHS, EDGE_PANELS),
            pltpu.VMEM((8, 128), jnp.int32),
        ]
        + [pltpu.VMEM((CLUSTER, CLUSTER), BF16)] * 4
        + [pltpu.SemaphoreType.DMA((count,)) for count in (4, 22, 22, 2, 4, 4, 7)],
        compiler_params=pltpu.CompilerParams(
            collective_id=0, has_side_effects=True, vmem_limit_bytes=60 * 2**20
        ),
    )(
        positions, weight, charges, basis, proxies, far_blocks, cross_pairs, local_pairs, cross_pairs, cross_count
    )
    self_sum, first_sum, second_sum, far_in, returned, info_in, proxy_table = outs
    return pl.pallas_call(
        far_kernel,
        out_shape=jax.ShapeDtypeStruct((RHS, panels), F32),
        in_specs=[hbm] * 12,
        out_specs=vmem,
        scratch_shapes=[
            floats(CL_DEV, 128),
            numbers(2, LOC_DEV),
            numbers(2, CROSS_DEV),
            numbers(1),
            numbers(8, 128),
            floats(CL_DEV, RHS, CLUSTER),
            floats(DEVICES * ROWS, 128),
            floats(RANK, panels),
            floats(1, panels),
            floats(CL_DEV, RHS, CLUSTER),
            floats(PAIRS, RHS, CLUSTER),
            floats(PAIRS, RHS, CLUSTER),
            floats(CROSS_DEV, RHS, CLUSTER),
            floats(128, FAR_DEV),
            floats(128, FAR_DEV),
            floats(RANK * RANK, FAR_DEV),
            floats(128, FAR_DEV),
            pltpu.SemaphoreType.DMA((12,)),
        ],
        compiler_params=pltpu.CompilerParams(vmem_limit_bytes=60 * 2**20),
    )(
        far_in.reshape(-1, 128), proxy_table, basis, weight, self_sum, first_sum, second_sum,
        returned, local_pairs, cross_pairs, cross_count, info_in,
    )


def solution(mesh):
    whole = P(None, ("gx", "gy"))
    flat = P(("gx", "gy"))
    return jax.shard_map(
        on_device,
        mesh=mesh,
        in_specs=(whole, flat, whole, whole, whole, whole, whole, flat, whole),
        out_specs=whole,
        check_vma=False,
    )
```

```python
import functools

import jax
import jax.numpy as jnp
from jax import lax
from jax.experimental import pallas as pl
from jax.experimental.pallas import tpu as pltpu
from jax.sharding import PartitionSpec as P

CLUSTER = 512
RANK = 16
RHS = 8
EDGE = 8
FOUR_PI_INV = 0.07957747154594767
SOFTENING = 0.0025
CL_DEV = 32
LOC_DEV = 32
CROSS_DEV = 16
PAIRS = CROSS_DEV + LOC_DEV
EARLY = 8
FAR_DEV = 256
EDGE_PANELS = EDGE * CLUSTER
SELF_CHUNK = 32
PAIR_CHUNK = 16
STRIP = 128
DEVICES = 128
N_Y, N_X, N_ZC = 4, 4, 8
ROWS = 8
MESH = pl.DeviceIdType.MESH
F32 = jnp.float32
BF16 = jnp.bfloat16


def dot(a, b, dims):
    return lax.dot_general(a, b, ((dims[:1], dims[1:]), ((), ())), preferred_element_type=F32)


def split(value, parts):
    out = []
    for _ in range(parts - 1):
        high = value.astype(BF16)
        out.append(high)
        value = value - high.astype(F32)
    out.append(value.astype(BF16))
    return out


def split_rows(value):
    high = value.astype(BF16).astype(F32)
    return jnp.concatenate([high, value - high], axis=0).astype(BF16)


def iotas(shape):
    return lax.broadcasted_iota(jnp.int32, shape, 0), lax.broadcasted_iota(jnp.int32, shape, 1)


def ones_where(condition):
    return jnp.where(condition, 1.0, 0.0).astype(BF16)


def cluster_cols(c):
    return slice(c * CLUSTER, (c + 1) * CLUSTER)


def near_kernel(
    pos_hbm, weight_hbm, charges_hbm, basis_hbm, proxies, far_blocks, cross_vector, local_pairs, cross_pairs, cross_count,
    self_out, first_out, second_out, far_in, returned, info_in, table_out,
    proxy_table, self_sum, first_sum, second_sum, pos, weight, charges, basis, cw, pos_c, pos_t, moments, coef_rows, proxy_rows, send, recv, head_w, next_pos, next_w,
    info, hi0, hi1, lo0, lo1, load_sem, far_send, far_recv, far_own, edge_send, edge_recv, out_sem,
):
    y = lax.axis_index("gx")
    gy = lax.axis_index("gy")
    x = gy // N_ZC
    zc = lax.rem(gy, N_ZC)
    flat = y * (N_X * N_ZC) + gy
    tile_hi, tile_lo = (hi0, hi1), (lo0, lo1)

    loads = [
        pltpu.make_async_copy(source, target, load_sem.at[i])
        for i, (source, target) in enumerate(
            ((weight_hbm, weight), (charges_hbm, charges), (pos_hbm, pos), (basis_hbm, basis))
        )
    ]
    for load in loads:
        load.start()

    def device_of(index):
        return (index // (N_X * N_ZC), lax.rem(index, N_X * N_ZC))

    after = device_of(lax.rem(flat + 1, DEVICES))
    before = device_of(lax.rem(flat + DEVICES - 1, DEVICES))
    chips = [(lax.rem(y + i // N_X, N_Y), lax.rem(x + i % N_X, N_X)) for i in range(1, N_Y * N_X)]
    peers = [(to_y, to_x * N_ZC + zc) for to_y, to_x in chips] + [
        (y, x * N_ZC + lax.rem(zc + i, N_ZC)) for i in range(1, N_ZC)
    ]
    barrier = pltpu.get_barrier_semaphore()
    for peer in peers + [after, before]:
        pl.semaphore_signal(barrier, inc=1, device_id=peer, device_id_type=MESH)

    info[...] = jnp.zeros_like(info)
    info[0:2, 0:CROSS_DEV] = cross_vector[...]
    info[2:3, :] = jnp.full((1, 128), cross_count[0], jnp.int32)

    columns = jnp.concatenate([proxies[...], jnp.zeros((5, CL_DEV * RANK), F32)], axis=0).T
    row, lane = iotas((CL_DEV * RANK, 128))
    spread = jnp.where(
        lane < RANK, columns[:, 0:1], jnp.where(lane < 2 * RANK, columns[:, 1:2], columns[:, 2:3])
    )
    spread = jnp.where((lax.rem(row, RANK) == lax.rem(lane, RANK)) & (lane < 3 * RANK), spread, 0.0)
    row, lane = iotas((CL_DEV, CL_DEV * RANK))
    gather = ones_where(row == lane // RANK)
    table = sum(dot(gather, part, (1, 0)) for part in split(spread, 3))
    proxy_table[...] = table
    out_table = pltpu.make_async_copy(proxy_table, table_out, out_sem.at[7])
    out_table.start()

    for load in loads:
        load.wait()
    for c in range(CL_DEV):
        cols = cluster_cols(c)
        parts = split_rows(charges[:, cols] * weight[:, cols])
        cw[c] = parts
        place = jnp.concatenate([pos[:, cols], jnp.zeros((5, CLUSTER), F32)], axis=0)
        pos_c[c] = place
        pos_t[c] = place.T
        moments[c * 32 : (c + 1) * 32, :] = dot(split_rows(basis[:, cols]), parts, (1, 1))
    head_w[...] = charges[:, :EDGE_PANELS] * weight[:, :EDGE_PANELS]

    row, lane = iotas((2 * RHS, 128))
    spread = ones_where(lax.rem(row, RHS) == lax.rem(lane, RHS))
    wide = sum(dot(part, spread, (1, 0)) for part in split(moments[...], 3))
    row, lane = iotas(wide.shape)
    wide = jnp.where(lax.rem(row, RANK) == lane // RHS, wide, 0.0)
    coef = jnp.sum(wide.reshape(CL_DEV, 2 * RANK, 128), axis=1)

    row, lane = iotas((CL_DEV, 256))
    numbers = jnp.where(lane == 128 + 3 * RANK, row.astype(F32), 0.0).astype(BF16)
    both = jnp.concatenate(split(jnp.concatenate([coef, table], axis=1), 3) + [numbers], axis=0)
    row, lane = iotas((3 * CL_DEV, FAR_DEV))
    pick_source = jnp.where(lax.rem(row, CL_DEV) == far_blocks[0:1, :], 1.0, 0.0)
    row, lane = iotas((CL_DEV, FAR_DEV))
    pick_number = jnp.where(row == (far_blocks[1:2, :] & (CL_DEV - 1)), 1.0, 0.0)
    pick = jnp.concatenate([pick_source, pick_number], axis=0).astype(BF16)
    picked = dot(pick, both, (0, 0))
    coef_rows[...] = picked[:, :128]
    proxy_rows[...] = picked[:, 128:]
    for j in range(2):
        send[pl.ds(j, DEVICES, stride=ROWS), :] = coef_rows[pl.ds(j, DEVICES, stride=2), :]
        for k in range(2, ROWS, 2):
            send[pl.ds(k + j, DEVICES, stride=ROWS), :] = proxy_rows[pl.ds(j, DEVICES, stride=2), :]

    def far_copy(source, target, index, peer):
        return pltpu.make_async_remote_copy(
            src_ref=source, dst_ref=target, send_sem=far_send.at[index], recv_sem=far_recv.at[index],
            device_id=peer, device_id_type=MESH,
        )

    def edge_copy(source, target, index, peer):
        return pltpu.make_async_remote_copy(
            src_ref=source, dst_ref=target, send_sem=edge_send.at[index], recv_sem=edge_recv.at[index],
            device_id=peer, device_id_type=MESH,
        )

    def start(copies):
        for copy in copies:
            copy.start()

    def wait(copies):
        for copy in copies:
            copy.wait()

    def part(index, count):
        return pl.ds(pl.multiple_of(index * count, count), count)

    per_chip = N_ZC * ROWS
    phase1 = [pltpu.make_async_copy(send.at[part(y * N_X + x, per_chip)], recv.at[0], far_own.at[0])] + [
        far_copy(send.at[part(to_y * N_X + to_x, per_chip)], recv.at[i + 1], i, peers[i])
        for i, (to_y, to_x) in enumerate(chips)
    ]
    phase2 = [pltpu.make_async_copy(recv.at[:, part(zc, ROWS)], far_in.at[0], far_own.at[1])] + [
        far_copy(recv.at[:, part(lax.rem(zc + i, N_ZC), ROWS)], far_in.at[i], len(chips) + i - 1, peers[len(chips) + i - 1])
        for i in range(1, N_ZC)
    ]
    heads = [
        edge_copy(pos.at[:, pl.ds(0, EDGE_PANELS)], next_pos, 0, before),
        edge_copy(head_w, next_w, 1, before),
        edge_copy(info, info_in, 2, after),
    ]
    crossing = pl.ds(EARLY, CROSS_DEV)
    give_back = edge_copy(second_sum.at[crossing], returned, 3, after)
    gives, gets = flat < DEVICES - 1, flat > 0

    def out_copies(index, first, count, *pairs):
        rows = pl.ds(first, count)
        return [
            pltpu.make_async_copy(source.at[rows], target.at[rows], out_sem.at[index + i])
            for i, (source, target) in enumerate(pairs)
        ]

    first_pair, second_pair = (first_sum, first_out), (second_sum, second_out)
    done = EARLY + CROSS_DEV
    outs_self = out_copies(0, 0, CL_DEV, (self_sum, self_out))
    outs_early = out_copies(1, 0, done, first_pair) + out_copies(2, 0, EARLY, second_pair)
    outs_late = out_copies(3, done, 16, first_pair, second_pair)
    outs_last = out_copies(5, done + 16, 8, first_pair, second_pair)

    def fill(row_cluster, columns, slot, row_from, row_to, col_from, chunk):
        col_x = pos_c[columns, 0:1, col_from:]
        col_y = pos_c[columns, 1:2, col_from:]
        col_z = pos_c[columns, 2:3, col_from:]
        for begin in range(row_from, row_to, chunk):
            rows = pos_t[row_cluster, begin : begin + chunk, :]
            dx = rows[:, 0:1] - col_x
            dy = rows[:, 1:2] - col_y
            dz = rows[:, 2:3] - col_z
            value = lax.rsqrt(dx * dx + dy * dy + dz * dz + SOFTENING)
            high = value.astype(BF16)
            tile_hi[slot][begin : begin + chunk, col_from:] = high
            tile_lo[slot][begin : begin + chunk, col_from:] = (value - high.astype(F32)).astype(BF16)

    def halves(parts, slot, rows, cols, side):
        sums = dot(parts, tile_hi[slot][rows, cols], (1, side)) + dot(parts, tile_lo[slot][rows, cols], (1, side))
        return sums[:RHS] + sums[RHS:]

    whole = slice(0, CLUSTER)

    def self_compute(t, slot):
        for begin in range(0, CLUSTER, STRIP):
            fill(t, t, slot, begin, begin + STRIP, begin, SELF_CHUNK)

    def self_apply(t, slot):
        parts = cw[t]
        sums = [None] * (CLUSTER // STRIP)
        for i in range(CLUSTER // STRIP):
            rows = slice(i * STRIP, (i + 1) * STRIP)
            down = halves(parts[:, rows], slot, rows, slice(i * STRIP, CLUSTER), 0)
            for j in range(i, CLUSTER // STRIP):
                piece = down[:, (j - i) * STRIP : (j - i + 1) * STRIP]
                sums[j] = piece if sums[j] is None else sums[j] + piece
            if i + 1 < CLUSTER // STRIP:
                rest = slice((i + 1) * STRIP, CLUSTER)
                sums[i] = sums[i] + halves(parts[:, rest], slot, rows, rest, 1)
        self_sum[t] = jnp.concatenate(sums, axis=1)

    def pair_of(t):
        crosses = (t >= EARLY) & (t < done)
        c = jnp.clip(t - EARLY, 0, CROSS_DEV - 1)
        l = jnp.clip(jnp.where(t < EARLY, t, t - CROSS_DEV), 0, LOC_DEV - 1)
        first = jnp.where(crosses, cross_pairs[0, c], local_pairs[0, l])
        second = jnp.where(crosses, cross_pairs[1, c] + CL_DEV, local_pairs[1, l])
        return first, second

    def pair_compute(t, slot):
        first, second = pair_of(t)
        fill(first, second, slot, 0, CLUSTER, 0, PAIR_CHUNK)

    def pair_apply(t, slot):
        first, second = pair_of(t)
        first_sum[t] = halves(cw[second], slot, whole, whole, 1)
        second_sum[t] = halves(cw[first], slot, whole, whole, 0)

    def section(count, compute, apply, steps, after):

        def body(i, carry):
            for at, step in steps:
                pl.when(i == at)(step)
            compute(2 * i + 1, 1)
            apply(2 * i, 0)
            compute(2 * i + 2, 0)
            apply(2 * i + 1, 1)
            return carry

        lax.fori_loop(0, count // 2 - 1, body, 0)
        compute(count - 1, 1)
        apply(count - 2, 0)
        after()
        apply(count - 1, 1)

    def send_first():
        pl.semaphore_wait(barrier, len(peers) + 2)
        start(heads)

    def take_heads():
        wait(heads)
        for j in range(EDGE):
            cw[CL_DEV + j] = split_rows(next_w[:, cluster_cols(j)])
            pos_c[CL_DEV + j, 0:3, :] = next_pos[:, cluster_cols(j)]

    def send_last():
        wait(phase1)
        start(phase2)

    def send_back():
        pl.when(gives)(give_back.start)
        start(outs_early)

    self_compute(0, 0)
    section(CL_DEV, self_compute, self_apply, [(6, send_first), (8, lambda: start(phase1))], lambda: pair_compute(0, 0))
    start(outs_self)
    section(
        PAIRS,
        pair_compute,
        pair_apply,
        [(EARLY // 2 - 1, take_heads), (8, send_last), (done // 2, send_back), (done // 2 + 8, lambda: start(outs_late))],
        lambda: None,
    )
    start(outs_last)
    out_table.wait()
    wait(outs_self)
    wait(outs_early)
    wait(outs_late)
    wait(phase2)
    pl.when(gives)(give_back.wait_send)
    pl.when(gets)(give_back.wait_recv)
    wait(outs_last)


def far_kernel(
    far_hbm, table_hbm, basis_hbm, weight_hbm, self_hbm, first_hbm, second_hbm, returned_hbm,
    local_hbm, cross_hbm, count_hbm, info_hbm,
    out, proxy_table, local_pairs, cross_pairs, cross_count, info_in, near, far_in, basis, weight, self_sum, first_sum, second_sum, returned, coef, target, coupling, contrib, load_sem,
):
    loads = [
        pltpu.make_async_copy(source, target, load_sem.at[i])
        for i, (source, target) in enumerate(
            (
                (far_hbm, far_in),
                (table_hbm, proxy_table),
                (basis_hbm, basis),
                (self_hbm, self_sum),
                (first_hbm, first_sum),
                (second_hbm, second_sum),
                (returned_hbm, returned),
                (weight_hbm, weight),
                (local_hbm, local_pairs),
                (cross_hbm, cross_pairs),
                (count_hbm, cross_count),
                (info_hbm, info_in),
            )
        )
    ]
    for load in loads:
        load.start()
    for load in loads[:2]:
        load.wait()

    def strided(j):
        return far_in[pl.ds(j, DEVICES, stride=ROWS), :]

    coef[...] = jnp.concatenate([strided(0).T, strided(1).T], axis=1)
    source = jnp.concatenate([strided(2).T, strided(3).T], axis=1)
    number = source[3 * RANK : 3 * RANK + 1, :].astype(jnp.int32)
    row, lane = iotas((CL_DEV, FAR_DEV))
    pick = ones_where(row == number)
    target[...] = sum(dot(part, pick, (0, 0)) for part in split(proxy_table[...], 3))
    for k in range(RANK):
        distance = SOFTENING
        for axis in range(3):
            end = axis * RANK + k
            offset = target[end : end + 1, :] - source[axis * RANK : (axis + 1) * RANK, :]
            distance = distance + offset * offset
        coupling[k * RANK : (k + 1) * RANK, :] = lax.rsqrt(distance)
    for k in range(RANK):
        total = None
        for l in range(RANK):
            entry = k * RANK + l
            term = coupling[entry : entry + 1, :] * coef[l * RHS : (l + 1) * RHS, :]
            total = term if total is None else total + term
        contrib[k * RHS : (k + 1) * RHS, :] = total
    rowcoef = sum(dot(pick, part, (1, 1)) for part in split(contrib[...], 3))
    row, lane = iotas((CL_DEV * RHS, CL_DEV))
    eight = ones_where(row // RHS == lane)
    wide = sum(dot(eight, part, (1, 0)) for part in split(rowcoef, 3))
    row, lane = iotas(wide.shape)
    wide = jnp.where(lax.rem(row, RHS) == lax.rem(lane, RHS), wide, 0.0)
    row, lane = iotas((128, RANK))
    narrow = ones_where(row // RHS == lane)
    rows = sum(dot(part, narrow, (1, 0)) for part in split(wide, 3))
    rows_high = rows.astype(BF16).astype(F32)
    lefts = jnp.concatenate([rows_high, rows_high, rows - rows_high], axis=1)
    for load in loads[2:]:
        load.wait()
    for c in range(CL_DEV):
        block = basis[:, cluster_cols(c)]
        high = block.astype(BF16).astype(F32)
        parts = jnp.concatenate([high, block - high, high], axis=0).astype(BF16)
        near[c] = self_sum[c] + dot(lefts[c * RHS : (c + 1) * RHS].astype(BF16), parts, (1, 0))

    def add_local(t, carry):
        slot = jnp.where(t < EARLY, t, t + CROSS_DEV)
        near[local_pairs[0, t]] += first_sum[slot]
        near[local_pairs[1, t]] += second_sum[slot]
        return carry

    lax.fori_loop(0, LOC_DEV, add_local, 0, unroll=8)

    def add_cross(t, carry):
        near[cross_pairs[0, t]] += first_sum[EARLY + t]
        return carry

    lax.fori_loop(0, cross_count[0], add_cross, 0)

    def add_returned(t, carry):
        near[info_in[1, t]] += returned[t]
        return carry

    lax.fori_loop(0, info_in[2, 0], add_returned, 0)
    for c in range(CL_DEV):
        cols = cluster_cols(c)
        out[:, cols] = near[c] * (weight[:, cols] * FOUR_PI_INV)


def on_device(
    positions, panel_weight, charges, basis, proxies, local_pairs, cross_pairs, cross_count, far_blocks
):
    panels = positions.shape[1]
    weight = panel_weight.reshape(1, panels)
    vmem = pl.BlockSpec(memory_space=pltpu.VMEM)
    smem = pl.BlockSpec(memory_space=pltpu.SMEM)
    hbm = pl.BlockSpec(memory_space=pltpu.HBM)

    def floats(*shape):
        return pltpu.VMEM(shape, F32)

    def numbers(*shape):
        return pltpu.SMEM(shape, jnp.int32)

    outs = pl.pallas_call(
        near_kernel,
        out_shape=[
            jax.ShapeDtypeStruct((CL_DEV, RHS, CLUSTER), F32),
            jax.ShapeDtypeStruct((PAIRS, RHS, CLUSTER), F32),
            jax.ShapeDtypeStruct((PAIRS, RHS, CLUSTER), F32),
            jax.ShapeDtypeStruct((N_ZC, N_Y * N_X, ROWS, 128), F32),
            jax.ShapeDtypeStruct((CROSS_DEV, RHS, CLUSTER), F32),
            jax.ShapeDtypeStruct((8, 128), jnp.int32),
            jax.ShapeDtypeStruct((CL_DEV, 128), F32),
        ],
        in_specs=[hbm] * 4 + [vmem] * 3 + [smem] * 3,
        out_specs=[hbm] * 7,
        scratch_shapes=[
            floats(CL_DEV, 128),
            floats(CL_DEV, RHS, CLUSTER),
            floats(PAIRS, RHS, CLUSTER),
            floats(PAIRS, RHS, CLUSTER),
            floats(3, panels),
            floats(1, panels),
            floats(RHS, panels),
            floats(RANK, panels),
            pltpu.VMEM((CL_DEV + EDGE, 2 * RHS, CLUSTER), BF16),
            floats(CL_DEV + EDGE, 8, CLUSTER),
            floats(CL_DEV, CLUSTER, 8),
            floats(CL_DEV * 2 * RANK, 2 * RHS),
            floats(FAR_DEV, 128),
            floats(FAR_DEV, 128),
            floats(DEVICES * ROWS, 128),
            floats(N_Y * N_X, N_ZC * ROWS, 128),
            floats(RHS, EDGE_PANELS),
            floats(3, EDGE_PANELS),
            floats(RHS, EDGE_PANELS),
            pltpu.VMEM((8, 128), jnp.int32),
        ]
        + [pltpu.VMEM((CLUSTER, CLUSTER), BF16)] * 4
        + [pltpu.SemaphoreType.DMA((count,)) for count in (4, 22, 22, 2, 4, 4, 8)],
        compiler_params=pltpu.CompilerParams(
            collective_id=0, has_side_effects=True, vmem_limit_bytes=60 * 2**20
        ),
    )(
        positions, weight, charges, basis, proxies, far_blocks, cross_pairs, local_pairs, cross_pairs, cross_count
    )
    self_sum, first_sum, second_sum, far_in, returned, info_in, proxy_table = outs
    return pl.pallas_call(
        far_kernel,
        out_shape=jax.ShapeDtypeStruct((RHS, panels), F32),
        in_specs=[hbm] * 12,
        out_specs=vmem,
        scratch_shapes=[
            floats(CL_DEV, 128),
            numbers(2, LOC_DEV),
            numbers(2, CROSS_DEV),
            numbers(1),
            numbers(8, 128),
            floats(CL_DEV, RHS, CLUSTER),
            floats(DEVICES * ROWS, 128),
            floats(RANK, panels),
            floats(1, panels),
            floats(CL_DEV, RHS, CLUSTER),
            floats(PAIRS, RHS, CLUSTER),
            floats(PAIRS, RHS, CLUSTER),
            floats(CROSS_DEV, RHS, CLUSTER),
            floats(128, FAR_DEV),
            floats(128, FAR_DEV),
            floats(RANK * RANK, FAR_DEV),
            floats(128, FAR_DEV),
            pltpu.SemaphoreType.DMA((12,)),
        ],
        compiler_params=pltpu.CompilerParams(vmem_limit_bytes=60 * 2**20),
    )(
        far_in.reshape(-1, 128), proxy_table, basis, weight, self_sum, first_sum, second_sum,
        returned, local_pairs, cross_pairs, cross_count, info_in,
    )


def solution(mesh):
    whole = P(None, ("gx", "gy"))
    flat = P(("gx", "gy"))
    return jax.shard_map(
        on_device,
        mesh=mesh,
        in_specs=(whole, flat, whole, whole, whole, whole, whole, flat, whole),
        out_specs=whole,
        check_vma=False,
    )
```

```python
import functools

import jax
import jax.numpy as jnp
from jax import lax
from jax.experimental import pallas as pl
from jax.experimental.pallas import tpu as pltpu
from jax.sharding import PartitionSpec as P

CLUSTER = 512
RANK = 16
RHS = 8
EDGE = 8
FOUR_PI_INV = 0.07957747154594767
SOFTENING = 0.0025
CL_DEV = 32
LOC_DEV = 32
CROSS_DEV = 16
PAIRS = CROSS_DEV + LOC_DEV
EARLY = 8
FAR_DEV = 256
EDGE_PANELS = EDGE * CLUSTER
SELF_CHUNK = 32
PAIR_CHUNK = 16
STRIP = 128
DEVICES = 128
N_Y, N_X, N_ZC = 4, 4, 8
ROWS = 8
MESH = pl.DeviceIdType.MESH
F32 = jnp.float32
BF16 = jnp.bfloat16


def dot(a, b, dims):
    return lax.dot_general(a, b, ((dims[:1], dims[1:]), ((), ())), preferred_element_type=F32)


def split(value, parts):
    out = []
    for _ in range(parts - 1):
        high = value.astype(BF16)
        out.append(high)
        value = value - high.astype(F32)
    out.append(value.astype(BF16))
    return out


def split_rows(value):
    high = value.astype(BF16).astype(F32)
    return jnp.concatenate([high, value - high], axis=0).astype(BF16)


def iotas(shape):
    return lax.broadcasted_iota(jnp.int32, shape, 0), lax.broadcasted_iota(jnp.int32, shape, 1)


def ones_where(condition):
    return jnp.where(condition, 1.0, 0.0).astype(BF16)


def cluster_cols(c):
    return slice(c * CLUSTER, (c + 1) * CLUSTER)


def near_kernel(
    pos_hbm, weight_hbm, charges_hbm, basis_hbm, proxies, far_blocks, cross_vector, local_pairs, cross_pairs, cross_count,
    self_out, first_out, second_out, far_in, returned, info_in, table_out,
    proxy_table, self_sum, first_sum, second_sum, pos, weight, charges, basis, cw, pos_c, pos_t, moments, coef_rows, proxy_rows, send, recv, head_w, next_pos, next_w,
    info, hi0, hi1, lo0, lo1, load_sem, far_send, far_recv, far_own, edge_send, edge_recv, out_sem,
):
    y = lax.axis_index("gx")
    gy = lax.axis_index("gy")
    x = gy // N_ZC
    zc = lax.rem(gy, N_ZC)
    flat = y * (N_X * N_ZC) + gy
    tile_hi, tile_lo = (hi0, hi1), (lo0, lo1)

    loads = [
        pltpu.make_async_copy(source, target, load_sem.at[i])
        for i, (source, target) in enumerate(
            ((pos_hbm, pos), (weight_hbm, weight), (charges_hbm, charges), (basis_hbm, basis))
        )
    ]
    for load in loads:
        load.start()

    def device_of(index):
        return (index // (N_X * N_ZC), lax.rem(index, N_X * N_ZC))

    after = device_of(lax.rem(flat + 1, DEVICES))
    before = device_of(lax.rem(flat + DEVICES - 1, DEVICES))
    chips = [(lax.rem(y + i // N_X, N_Y), lax.rem(x + i % N_X, N_X)) for i in range(1, N_Y * N_X)]
    peers = [(to_y, to_x * N_ZC + zc) for to_y, to_x in chips] + [
        (y, x * N_ZC + lax.rem(zc + i, N_ZC)) for i in range(1, N_ZC)
    ]
    barrier = pltpu.get_barrier_semaphore()
    for peer in peers + [after, before]:
        pl.semaphore_signal(barrier, inc=1, device_id=peer, device_id_type=MESH)

    info[...] = jnp.zeros_like(info)
    info[0:2, 0:CROSS_DEV] = cross_vector[...]
    info[2:3, :] = jnp.full((1, 128), cross_count[0], jnp.int32)

    columns = jnp.concatenate([proxies[...], jnp.zeros((5, CL_DEV * RANK), F32)], axis=0).T
    row, lane = iotas((CL_DEV * RANK, 128))
    spread = jnp.where(
        lane < RANK, columns[:, 0:1], jnp.where(lane < 2 * RANK, columns[:, 1:2], columns[:, 2:3])
    )
    spread = jnp.where((lax.rem(row, RANK) == lax.rem(lane, RANK)) & (lane < 3 * RANK), spread, 0.0)
    row, lane = iotas((CL_DEV, CL_DEV * RANK))
    gather = ones_where(row == lane // RANK)
    table = sum(dot(gather, part, (1, 0)) for part in split(spread, 3))
    proxy_table[...] = table
    out_table = pltpu.make_async_copy(proxy_table, table_out, out_sem.at[7])
    out_table.start()

    for load in loads[:3]:
        load.wait()
    for c in range(CL_DEV):
        cols = cluster_cols(c)
        parts = split_rows(charges[:, cols] * weight[:, cols])
        cw[c] = parts
        place = jnp.concatenate([pos[:, cols], jnp.zeros((5, CLUSTER), F32)], axis=0)
        pos_c[c] = place
        pos_t[c] = place.T
    head_w[...] = charges[:, :EDGE_PANELS] * weight[:, :EDGE_PANELS]
    loads[3].wait()
    for c in range(CL_DEV):
        moments[c * 32 : (c + 1) * 32, :] = dot(split_rows(basis[:, cluster_cols(c)]), cw[c], (1, 1))

    row, lane = iotas((2 * RHS, 128))
    spread = ones_where(lax.rem(row, RHS) == lax.rem(lane, RHS))
    wide = sum(dot(part, spread, (1, 0)) for part in split(moments[...], 3))
    row, lane = iotas(wide.shape)
    wide = jnp.where(lax.rem(row, RANK) == lane // RHS, wide, 0.0)
    coef = jnp.sum(wide.reshape(CL_DEV, 2 * RANK, 128), axis=1)

    row, lane = iotas((CL_DEV, 256))
    numbers = jnp.where(lane == 128 + 3 * RANK, row.astype(F32), 0.0).astype(BF16)
    both = jnp.concatenate(split(jnp.concatenate([coef, table], axis=1), 3) + [numbers], axis=0)
    row, lane = iotas((3 * CL_DEV, FAR_DEV))
    pick_source = jnp.where(lax.rem(row, CL_DEV) == far_blocks[0:1, :], 1.0, 0.0)
    row, lane = iotas((CL_DEV, FAR_DEV))
    pick_number = jnp.where(row == (far_blocks[1:2, :] & (CL_DEV - 1)), 1.0, 0.0)
    pick = jnp.concatenate([pick_source, pick_number], axis=0).astype(BF16)
    picked = dot(pick, both, (0, 0))
    coef_rows[...] = picked[:, :128]
    proxy_rows[...] = picked[:, 128:]
    for j in range(2):
        send[pl.ds(j, DEVICES, stride=ROWS), :] = coef_rows[pl.ds(j, DEVICES, stride=2), :]
        for k in range(2, ROWS, 2):
            send[pl.ds(k + j, DEVICES, stride=ROWS), :] = proxy_rows[pl.ds(j, DEVICES, stride=2), :]

    def far_copy(source, target, index, peer):
        return pltpu.make_async_remote_copy(
            src_ref=source, dst_ref=target, send_sem=far_send.at[index], recv_sem=far_recv.at[index],
            device_id=peer, device_id_type=MESH,
        )

    def edge_copy(source, target, index, peer):
        return pltpu.make_async_remote_copy(
            src_ref=source, dst_ref=target, send_sem=edge_send.at[index], recv_sem=edge_recv.at[index],
            device_id=peer, device_id_type=MESH,
        )

    def start(copies):
        for copy in copies:
            copy.start()

    def wait(copies):
        for copy in copies:
            copy.wait()

    def part(index, count):
        return pl.ds(pl.multiple_of(index * count, count), count)

    per_chip = N_ZC * ROWS
    phase1 = [pltpu.make_async_copy(send.at[part(y * N_X + x, per_chip)], recv.at[0], far_own.at[0])] + [
        far_copy(send.at[part(to_y * N_X + to_x, per_chip)], recv.at[i + 1], i, peers[i])
        for i, (to_y, to_x) in enumerate(chips)
    ]
    phase2 = [pltpu.make_async_copy(recv.at[:, part(zc, ROWS)], far_in.at[0], far_own.at[1])] + [
        far_copy(recv.at[:, part(lax.rem(zc + i, N_ZC), ROWS)], far_in.at[i], len(chips) + i - 1, peers[len(chips) + i - 1])
        for i in range(1, N_ZC)
    ]
    heads = [
        edge_copy(pos.at[:, pl.ds(0, EDGE_PANELS)], next_pos, 0, before),
        edge_copy(head_w, next_w, 1, before),
        edge_copy(info, info_in, 2, after),
    ]
    crossing = pl.ds(EARLY, CROSS_DEV)
    give_back = edge_copy(second_sum.at[crossing], returned, 3, after)
    gives, gets = flat < DEVICES - 1, flat > 0

    def out_copies(index, first, count, *pairs):
        rows = pl.ds(first, count)
        return [
            pltpu.make_async_copy(source.at[rows], target.at[rows], out_sem.at[index + i])
            for i, (source, target) in enumerate(pairs)
        ]

    first_pair, second_pair = (first_sum, first_out), (second_sum, second_out)
    done = EARLY + CROSS_DEV
    outs_self = out_copies(0, 0, CL_DEV, (self_sum, self_out))
    outs_early = out_copies(1, 0, done, first_pair) + out_copies(2, 0, EARLY, second_pair)
    outs_late = out_copies(3, done, 16, first_pair, second_pair)
    outs_last = out_copies(5, done + 16, 8, first_pair, second_pair)

    def fill(row_cluster, columns, slot, row_from, row_to, col_from, chunk):
        col_x = pos_c[columns, 0:1, col_from:]
        col_y = pos_c[columns, 1:2, col_from:]
        col_z = pos_c[columns, 2:3, col_from:]
        for begin in range(row_from, row_to, chunk):
            rows = pos_t[row_cluster, begin : begin + chunk, :]
            dx = rows[:, 0:1] - col_x
            dy = rows[:, 1:2] - col_y
            dz = rows[:, 2:3] - col_z
            value = lax.rsqrt(dx * dx + dy * dy + dz * dz + SOFTENING)
            high = value.astype(BF16)
            tile_hi[slot][begin : begin + chunk, col_from:] = high
            tile_lo[slot][begin : begin + chunk, col_from:] = (value - high.astype(F32)).astype(BF16)

    def halves(parts, slot, rows, cols, side):
        sums = dot(parts, tile_hi[slot][rows, cols], (1, side)) + dot(parts, tile_lo[slot][rows, cols], (1, side))
        return sums[:RHS] + sums[RHS:]

    whole = slice(0, CLUSTER)

    def self_compute(t, slot):
        for begin in range(0, CLUSTER, STRIP):
            fill(t, t, slot, begin, begin + STRIP, begin, SELF_CHUNK)

    def self_apply(t, slot):
        parts = cw[t]
        sums = [None] * (CLUSTER // STRIP)
        for i in range(CLUSTER // STRIP):
            rows = slice(i * STRIP, (i + 1) * STRIP)
            down = halves(parts[:, rows], slot, rows, slice(i * STRIP, CLUSTER), 0)
            for j in range(i, CLUSTER // STRIP):
                piece = down[:, (j - i) * STRIP : (j - i + 1) * STRIP]
                sums[j] = piece if sums[j] is None else sums[j] + piece
            if i + 1 < CLUSTER // STRIP:
                rest = slice((i + 1) * STRIP, CLUSTER)
                sums[i] = sums[i] + halves(parts[:, rest], slot, rows, rest, 1)
        self_sum[t] = jnp.concatenate(sums, axis=1)

    def pair_of(t):
        crosses = (t >= EARLY) & (t < done)
        c = jnp.clip(t - EARLY, 0, CROSS_DEV - 1)
        l = jnp.clip(jnp.where(t < EARLY, t, t - CROSS_DEV), 0, LOC_DEV - 1)
        first = jnp.where(crosses, cross_pairs[0, c], local_pairs[0, l])
        second = jnp.where(crosses, cross_pairs[1, c] + CL_DEV, local_pairs[1, l])
        return first, second

    def pair_compute(t, slot):
        first, second = pair_of(t)
        fill(first, second, slot, 0, CLUSTER, 0, PAIR_CHUNK)

    def pair_apply(t, slot):
        first, second = pair_of(t)
        first_sum[t] = halves(cw[second], slot, whole, whole, 1)
        second_sum[t] = halves(cw[first], slot, whole, whole, 0)

    def section(count, compute, apply, steps, after):

        def body(i, carry):
            for at, step in steps:
                pl.when(i == at)(step)
            compute(2 * i + 1, 1)
            apply(2 * i, 0)
            compute(2 * i + 2, 0)
            apply(2 * i + 1, 1)
            return carry

        lax.fori_loop(0, count // 2 - 1, body, 0)
        compute(count - 1, 1)
        apply(count - 2, 0)
        after()
        apply(count - 1, 1)

    def send_first():
        pl.semaphore_wait(barrier, len(peers) + 2)
        start(heads)

    def take_heads():
        wait(heads)
        for j in range(EDGE):
            cw[CL_DEV + j] = split_rows(next_w[:, cluster_cols(j)])
            pos_c[CL_DEV + j, 0:3, :] = next_pos[:, cluster_cols(j)]

    def send_last():
        wait(phase1)
        start(phase2)

    def send_back():
        pl.when(gives)(give_back.start)
        start(outs_early)

    self_compute(0, 0)
    section(CL_DEV, self_compute, self_apply, [(6, send_first), (8, lambda: start(phase1))], lambda: pair_compute(0, 0))
    start(outs_self)
    section(
        PAIRS,
        pair_compute,
        pair_apply,
        [(EARLY // 2 - 1, take_heads), (8, send_last), (done // 2, send_back), (done // 2 + 8, lambda: start(outs_late))],
        lambda: None,
    )
    start(outs_last)
    out_table.wait()
    wait(outs_self)
    wait(outs_early)
    wait(outs_late)
    wait(phase2)
    pl.when(gives)(give_back.wait_send)
    pl.when(gets)(give_back.wait_recv)
    wait(outs_last)


def far_kernel(
    far_hbm, table_hbm, basis_hbm, weight_hbm, self_hbm, first_hbm, second_hbm, returned_hbm,
    local_hbm, cross_hbm, count_hbm, info_hbm,
    out, proxy_table, local_pairs, cross_pairs, cross_count, info_in, near, far_in, basis, weight, self_sum, first_sum, second_sum, returned, coef, target, coupling, contrib, load_sem,
):
    loads = [
        pltpu.make_async_copy(source, target, load_sem.at[i])
        for i, (source, target) in enumerate(
            (
                (far_hbm, far_in),
                (table_hbm, proxy_table),
                (basis_hbm, basis),
                (self_hbm, self_sum),
                (first_hbm, first_sum),
                (second_hbm, second_sum),
                (returned_hbm, returned),
                (weight_hbm, weight),
                (local_hbm, local_pairs),
                (cross_hbm, cross_pairs),
                (count_hbm, cross_count),
                (info_hbm, info_in),
            )
        )
    ]
    for load in loads:
        load.start()
    for load in loads[:2]:
        load.wait()

    def strided(j):
        return far_in[pl.ds(j, DEVICES, stride=ROWS), :]

    coef[...] = jnp.concatenate([strided(0).T, strided(1).T], axis=1)
    source = jnp.concatenate([strided(2).T, strided(3).T], axis=1)
    number = source[3 * RANK : 3 * RANK + 1, :].astype(jnp.int32)
    row, lane = iotas((CL_DEV, FAR_DEV))
    pick = ones_where(row == number)
    target[...] = sum(dot(part, pick, (0, 0)) for part in split(proxy_table[...], 3))
    for k in range(RANK):
        distance = SOFTENING
        for axis in range(3):
            end = axis * RANK + k
            offset = target[end : end + 1, :] - source[axis * RANK : (axis + 1) * RANK, :]
            distance = distance + offset * offset
        coupling[k * RANK : (k + 1) * RANK, :] = lax.rsqrt(distance)
    for k in range(RANK):
        total = None
        for l in range(RANK):
            entry = k * RANK + l
            term = coupling[entry : entry + 1, :] * coef[l * RHS : (l + 1) * RHS, :]
            total = term if total is None else total + term
        contrib[k * RHS : (k + 1) * RHS, :] = total
    rowcoef = sum(dot(pick, part, (1, 1)) for part in split(contrib[...], 3))
    row, lane = iotas((CL_DEV * RHS, CL_DEV))
    eight = ones_where(row // RHS == lane)
    wide = sum(dot(eight, part, (1, 0)) for part in split(rowcoef, 3))
    row, lane = iotas(wide.shape)
    wide = jnp.where(lax.rem(row, RHS) == lax.rem(lane, RHS), wide, 0.0)
    row, lane = iotas((128, RANK))
    narrow = ones_where(row // RHS == lane)
    rows = sum(dot(part, narrow, (1, 0)) for part in split(wide, 3))
    rows_high = rows.astype(BF16).astype(F32)
    lefts = jnp.concatenate([rows_high, rows_high, rows - rows_high], axis=1)
    for load in loads[2:]:
        load.wait()
    for c in range(CL_DEV):
        block = basis[:, cluster_cols(c)]
        high = block.astype(BF16).astype(F32)
        parts = jnp.concatenate([high, block - high, high], axis=0).astype(BF16)
        near[c] = self_sum[c] + dot(lefts[c * RHS : (c + 1) * RHS].astype(BF16), parts, (1, 0))

    def add_local(t, carry):
        slot = jnp.where(t < EARLY, t, t + CROSS_DEV)
        near[local_pairs[0, t]] += first_sum[slot]
        near[local_pairs[1, t]] += second_sum[slot]
        return carry

    lax.fori_loop(0, LOC_DEV, add_local, 0, unroll=8)

    def add_cross(t, carry):
        near[cross_pairs[0, t]] += first_sum[EARLY + t]
        return carry

    lax.fori_loop(0, cross_count[0], add_cross, 0)

    def add_returned(t, carry):
        near[info_in[1, t]] += returned[t]
        return carry

    lax.fori_loop(0, info_in[2, 0], add_returned, 0)
    for c in range(CL_DEV):
        cols = cluster_cols(c)
        out[:, cols] = near[c] * (weight[:, cols] * FOUR_PI_INV)


def on_device(
    positions, panel_weight, charges, basis, proxies, local_pairs, cross_pairs, cross_count, far_blocks
):
    panels = positions.shape[1]
    weight = panel_weight.reshape(1, panels)
    vmem = pl.BlockSpec(memory_space=pltpu.VMEM)
    smem = pl.BlockSpec(memory_space=pltpu.SMEM)
    hbm = pl.BlockSpec(memory_space=pltpu.HBM)

    def floats(*shape):
        return pltpu.VMEM(shape, F32)

    def numbers(*shape):
        return pltpu.SMEM(shape, jnp.int32)

    outs = pl.pallas_call(
        near_kernel,
        out_shape=[
            jax.ShapeDtypeStruct((CL_DEV, RHS, CLUSTER), F32),
            jax.ShapeDtypeStruct((PAIRS, RHS, CLUSTER), F32),
            jax.ShapeDtypeStruct((PAIRS, RHS, CLUSTER), F32),
            jax.ShapeDtypeStruct((N_ZC, N_Y * N_X, ROWS, 128), F32),
            jax.ShapeDtypeStruct((CROSS_DEV, RHS, CLUSTER), F32),
            jax.ShapeDtypeStruct((8, 128), jnp.int32),
            jax.ShapeDtypeStruct((CL_DEV, 128), F32),
        ],
        in_specs=[hbm] * 4 + [vmem] * 3 + [smem] * 3,
        out_specs=[hbm] * 7,
        scratch_shapes=[
            floats(CL_DEV, 128),
            floats(CL_DEV, RHS, CLUSTER),
            floats(PAIRS, RHS, CLUSTER),
            floats(PAIRS, RHS, CLUSTER),
            floats(3, panels),
            floats(1, panels),
            floats(RHS, panels),
            floats(RANK, panels),
            pltpu.VMEM((CL_DEV + EDGE, 2 * RHS, CLUSTER), BF16),
            floats(CL_DEV + EDGE, 8, CLUSTER),
            floats(CL_DEV, CLUSTER, 8),
            floats(CL_DEV * 2 * RANK, 2 * RHS),
            floats(FAR_DEV, 128),
            floats(FAR_DEV, 128),
            floats(DEVICES * ROWS, 128),
            floats(N_Y * N_X, N_ZC * ROWS, 128),
            floats(RHS, EDGE_PANELS),
            floats(3, EDGE_PANELS),
            floats(RHS, EDGE_PANELS),
            pltpu.VMEM((8, 128), jnp.int32),
        ]
        + [pltpu.VMEM((CLUSTER, CLUSTER), BF16)] * 4
        + [pltpu.SemaphoreType.DMA((count,)) for count in (4, 22, 22, 2, 4, 4, 8)],
        compiler_params=pltpu.CompilerParams(
            collective_id=0, has_side_effects=True, vmem_limit_bytes=60 * 2**20
        ),
    )(
        positions, weight, charges, basis, proxies, far_blocks, cross_pairs, local_pairs, cross_pairs, cross_count
    )
    self_sum, first_sum, second_sum, far_in, returned, info_in, proxy_table = outs
    return pl.pallas_call(
        far_kernel,
        out_shape=jax.ShapeDtypeStruct((RHS, panels), F32),
        in_specs=[hbm] * 12,
        out_specs=vmem,
        scratch_shapes=[
            floats(CL_DEV, 128),
            numbers(2, LOC_DEV),
            numbers(2, CROSS_DEV),
            numbers(1),
            numbers(8, 128),
            floats(CL_DEV, RHS, CLUSTER),
            floats(DEVICES * ROWS, 128),
            floats(RANK, panels),
            floats(1, panels),
            floats(CL_DEV, RHS, CLUSTER),
            floats(PAIRS, RHS, CLUSTER),
            floats(PAIRS, RHS, CLUSTER),
            floats(CROSS_DEV, RHS, CLUSTER),
            floats(128, FAR_DEV),
            floats(128, FAR_DEV),
            floats(RANK * RANK, FAR_DEV),
            floats(128, FAR_DEV),
            pltpu.SemaphoreType.DMA((12,)),
        ],
        compiler_params=pltpu.CompilerParams(vmem_limit_bytes=60 * 2**20),
    )(
        far_in.reshape(-1, 128), proxy_table, basis, weight, self_sum, first_sum, second_sum,
        returned, local_pairs, cross_pairs, cross_count, info_in,
    )


def solution(mesh):
    whole = P(None, ("gx", "gy"))
    flat = P(("gx", "gy"))
    return jax.shard_map(
        on_device,
        mesh=mesh,
        in_specs=(whole, flat, whole, whole, whole, whole, whole, flat, whole),
        out_specs=whole,
        check_vma=False,
    )
```
